128 devices in a mesh: replica: 4 (over x), shard: 32 (over z, y, core).
Axes of the slice: x: 4, y: 4, z: 4, core: 2. Of those that a mesh axis runs over, the one named last changes fastest.
Arguments:
- pseudo_grad: bfloat16 [4, 4096, 8192], P('replica', 'shard'), may hold values from -36 to 36
- error_buf: bfloat16 [4, 4096, 8192], P('replica', 'shard'), may hold values from -3 to 3
- momentum: bfloat16 [4096, 8192], P('shard'), may hold values from -3 to 3
- params: float32 [4096, 8192], P('shard'), may hold values from -6 to 6
- right_factor: float32 [8192, 128], P('shard'), may hold values from -0.0625 to 0.0625
Outputs:
- new_error: bfloat16 [4, 4096, 8192], P('replica', 'shard')
- new_momentum: bfloat16 [4096, 8192], P('shard')
- new_params: float32 [4096, 8192], P('shard')
- new_right: float32 [8192, 128], P('shard')
The draws below stay inside these ranges and needn't reach their ends.
All inputs are finite; a program needn't handle non-finite values.
Results may differ from the reference program's by a relative error of at most 0.0012.
Values sent between devices are 32-bit elements; how exact they have to be, the bound alone decides.
No kernel may reach another device: no remote copies, remote signals or barrier semaphores. Data moves between devices by JAX's collectives and lax.ppermute only.
A program may use at most 128 MiB of HBM per device.

```python
import math
import jax
import jax.numpy as jnp
from jax import lax

ROWS = 4096
COLS = 8192
RANK = 128
REPLICAS = 4


def draw_pseudo_grad(key, part):
    key = jax.random.fold_in(key, 7)
    key_rows, key_cols, key_main = jax.random.split(key, 3)
    low = math.log(0.3)
    high = math.log(3.0)
    row_scale = jnp.exp(jax.random.uniform(key_rows, (REPLICAS, ROWS, 1), jnp.float32, low, high))
    col_scale = jnp.exp(jax.random.uniform(key_cols, (1, 1, COLS), jnp.float32, low, high))
    noise = jnp.clip(jax.random.normal(key_main, (REPLICAS, ROWS, COLS), jnp.float32), -4.0, 4.0)
    return (noise * row_scale * col_scale).astype(jnp.bfloat16)


def block_levels(stream_key, extent, pieces, least, high):
    def one(dim, shards_of):
        steps = jax.random.uniform(jax.random.fold_in(jax.random.fold_in(stream_key, 6), dim), (shards_of,), jnp.float32, least / len(pieces), high / len(pieces))
        return jnp.repeat(jnp.exp(steps), extent[dim] // shards_of).reshape((-1,) + (1,) * (len(extent) - dim - 1))

    level = one(*pieces[0])
    for cut in pieces[1:]:
        level = level * one(*cut)
    return level


def normal_values(stream_key, dims, spread, most, cuts=(), kind=jnp.bfloat16):
    factor_of = block_levels(stream_key, dims, cuts, -0.22, 0.18) if cuts else 1.0
    drawn = jax.random.normal(stream_key, dims, jnp.float32) * spread * factor_of
    return jnp.minimum(jnp.maximum(drawn, -most), most).astype(kind)


def setup_inputs(seed: int = 0) -> dict:
    splits = jax.random.split(jax.random.key(seed), 6)
    pseudo_grad = draw_pseudo_grad(jax.random.fold_in(splits[5], 71), 0)
    error_buf = normal_values(splits[1], (REPLICAS, ROWS, COLS), 0.5, 3.0, ((0, 4), (1, 32)))
    momentum = normal_values(splits[2], (ROWS, COLS), 0.5, 3.0, ((0, 32),))
    params = normal_values(splits[3], (ROWS, COLS), 1.0, 6.0, ((0, 32),), jnp.float32)
    right_factor = normal_values(splits[4], (COLS, RANK), COLS ** -0.5, 0.0625, ((0, 32),), jnp.float32)
    return {"pseudo_grad": pseudo_grad, "error_buf": error_buf, "momentum": momentum, "params": params, "right_factor": right_factor}


def reference(pseudo_grad, error_buf, momentum, params, right_factor):
    high = lax.Precision.HIGHEST
    merged = pseudo_grad.astype(jnp.float32) + error_buf.astype(jnp.float32)
    left = jnp.einsum('rij,jk->rik', merged, right_factor, precision=high).sum(0) / REPLICAS
    gram = jnp.dot(left.T.astype(jnp.float32), left.astype(jnp.float32), precision=high, preferred_element_type=jnp.float32)
    gram = gram + 1e-06 * jnp.trace(gram) / RANK * jnp.eye(RANK, dtype=jnp.float32)
    lower = jnp.linalg.cholesky(gram)
    basis = lax.linalg.triangular_solve(lower, left, left_side=False, lower=True, transpose_a=True)
    new_right = jnp.einsum('rij,ik->rjk', merged, basis, precision=high).sum(0) / REPLICAS
    approx = jnp.dot(basis.astype(jnp.float32), new_right.T.astype(jnp.float32), precision=high, preferred_element_type=jnp.float32)
    new_error = (merged - approx[None]).astype(jnp.bfloat16)
    moment = 0.9 * momentum.astype(jnp.float32) + approx
    new_params = params - 0.7 * (approx + 0.9 * moment)
    return (new_error, moment.astype(jnp.bfloat16), new_params, new_right)
```

```python
import jax
import jax.numpy as jnp
from jax import lax
from jax.experimental import pallas as pl
from jax.experimental.pallas import tpu as pltpu
from jax.sharding import Mesh, PartitionSpec as P

F32 = jnp.float32
BF16 = jnp.bfloat16
HIGH = lax.Precision.HIGHEST
CHIPS = ("x", "z", "y")
PLANE = ("z", "y")
VMEM = pl.BlockSpec(memory_space=pltpu.VMEM)
SMEM = pl.BlockSpec(memory_space=pltpu.SMEM)


def split(value):
    high = value.astype(BF16)
    return high, (value - high.astype(F32)).astype(BF16)


def dot(a, b):
    return jnp.dot(a, b, preferred_element_type=F32)


def ring(array, axis, step):
    n = lax.axis_size(axis)
    return lax.ppermute(array, axis, [(i, (i + step) % n) for i in range(n)])


def exchange(array, axis):
    return array, ring(array, axis, 2), ring(array, axis, 1), ring(array, axis, -1)


def total(parts):
    return (parts[0] + parts[1]) + (parts[2] + parts[3])


def call(kernel, out_shape, in_specs, out_specs, **kwargs):
    return pl.pallas_call(
        kernel,
        out_shape=out_shape,
        in_specs=in_specs,
        out_specs=out_specs,
        compiler_params=pltpu.CompilerParams(vmem_limit_bytes=48 << 20),
        **kwargs,
    )


def left_kernel(core, grad, error, mine, other, out):
    acc = jnp.zeros((256, 256), F32)
    for piece in range(mine.shape[0]):
        for source, owner in ((mine, core[0]), (other, 1 - core[0])):
            high, low = split(source[piece])
            cols = pl.ds(pl.multiple_of(piece * 512 + owner * 256, 256), 256)
            rows = jnp.concatenate([grad[0, :, cols], error[0, :, cols]], 0)
            acc += dot(rows, jnp.concatenate([high, low], 1))
    acc = acc[:128] + acc[128:]
    out[...] = acc[:, :128] + acc[:, 128:]


def raw_rows(half, parts, grad, error, left_t, store):
    left = total([part[...] for part in parts]) * 0.25
    left_t[...] = left.T
    high, low = split(left_t[pl.ds(pl.multiple_of(half * 64, 64), 64), :])
    rows = jnp.concatenate([high, low], 0)
    rows = jnp.concatenate([rows, rows], 1)
    for piece in range(32):
        cols = slice(piece * 256, piece * 256 + 256)
        block = dot(rows, jnp.concatenate([grad[0, :, cols], error[0, :, cols]], 0))
        block = block[:64] + block[64:]
        store(2 * piece, block[:, :128])
        store(2 * piece + 1, block[:, 128:])
    return left


def away_kernel(core, p0, p1, p2, p3, grad, error, out, left_out, gram, left_t):
    def store(index, block):
        out[index] = block

    left = raw_rows(1 - core[0], (p0, p1, p2, p3), grad, error, left_t, store)
    left_out[...] = left
    gram[...] = lax.dot(left_t[...], left, precision=HIGH, preferred_element_type=F32)


def home_kernel(core, p0, p1, p2, p3, grad, error, came, out, left_t):
    def store(index, block):
        out[index] = block + came[index]

    raw_rows(core[0], (p0, p1, p2, p3), grad, error, left_t, store)


def sum_kernel(parts, out):
    whole = jnp.sum(parts[...], 0) * 0.25
    for piece in range(out.shape[0]):
        out[piece] = whole


def last_kernel(core, factor, mine, other, grad, error, momentum, params, new_error, new_momentum, new_params):
    weights = factor[...]
    weights = jnp.where(core[0] == 0, weights, pltpu.roll(weights, 64, 1))
    high, low = split(weights)
    rows = jnp.concatenate(
        [jnp.concatenate([high, high], 1), jnp.concatenate([low, jnp.zeros_like(low)], 1)], 0
    )
    for piece in range(mine.shape[0] // 2):
        raw = jnp.concatenate(
            [
                jnp.concatenate([mine[2 * piece], mine[2 * piece + 1]], 1),
                jnp.concatenate([other[2 * piece], other[2 * piece + 1]], 1),
            ],
            0,
        )
        approx = dot(rows, jnp.concatenate(split(raw), 0))
        approx = approx[:128] + approx[128:]
        cols = slice(piece * 256, piece * 256 + 256)
        merged = grad[0, :, cols].astype(F32) + error[0, :, cols].astype(F32)
        new_error[0, :, cols] = (merged - approx).astype(BF16)
        moment = 0.9 * momentum[:, cols].astype(F32) + approx
        new_momentum[:, cols] = moment.astype(BF16)
        new_params[:, cols] = params[:, cols] - 0.7 * (approx + 0.9 * moment)


def local(pseudo_grad, error_buf, momentum, params, right_factor):
    core_index = lax.axis_index("core")
    core = core_index.astype(jnp.int32).reshape(1)
    square = jax.ShapeDtypeStruct((128, 128), F32)
    blocks = jax.ShapeDtypeStruct((64, 64, 128), F32)

    copies = jnp.broadcast_to(right_factor[None], (16, 256, 128))
    mine = lax.all_to_all(copies, PLANE, 0, 0)
    other = ring(mine, "core", 1)
    part = call(left_kernel, square, [SMEM] + [VMEM] * 4, VMEM)(core, pseudo_grad, error_buf, mine, other)

    parts = exchange(part, "x")
    scratch = [pltpu.VMEM((128, 128), F32)]
    away, left, gram = call(
        away_kernel, (blocks, square, square), [SMEM] + [VMEM] * 6, (VMEM,) * 3, scratch_shapes=scratch
    )(core, *parts, pseudo_grad, error_buf)
    came = ring(away, "core", 1)
    home = call(home_kernel, blocks, [SMEM] + [VMEM] * 7, VMEM, scratch_shapes=scratch)(
        core, *parts, pseudo_grad, error_buf, came
    )
    shares = lax.all_to_all(home, CHIPS, 0, 0)
    raw_copies = call(sum_kernel, blocks, [VMEM], VMEM)(shares)
    raw_mine = lax.all_to_all(raw_copies, CHIPS, 0, 0)
    raw_other = ring(raw_mine, "core", 1)

    gram = gram + ring(gram, "core", 1)
    gram = total(exchange(gram, "y"))
    gram = total(exchange(gram, "z"))
    eye = jnp.eye(128, dtype=F32)
    gram = gram + 1e-06 * jnp.trace(gram) / 128 * eye
    lower = jnp.linalg.cholesky(gram)
    inverse = lax.linalg.triangular_solve(lower, eye, left_side=True, lower=True)
    factor = jnp.dot(jnp.dot(left, inverse.T, precision=HIGH), inverse, precision=HIGH)

    n = 8
    wide = 8192 // n
    strip3 = pl.BlockSpec((1, 128, wide), lambda i: (0, 0, i))
    strip = pl.BlockSpec((128, wide), lambda i: (0, i))
    raw_spec = pl.BlockSpec((64 // n, 64, 128), lambda i: (i, 0, 0))
    whole = pl.BlockSpec((128, 128), lambda i: (0, 0))
    new_error, new_momentum, new_params = call(
        last_kernel,
        (
            jax.ShapeDtypeStruct(error_buf.shape, BF16),
            jax.ShapeDtypeStruct(momentum.shape, BF16),
            jax.ShapeDtypeStruct(params.shape, F32),
        ),
        [SMEM, whole, raw_spec, raw_spec, strip3, strip3, strip, strip],
        (strip3, strip, strip),
        grid=(n,),
    )(core, factor, raw_mine, raw_other, pseudo_grad, error_buf, momentum, params)

    shard = (lax.axis_index("z") * 4 + lax.axis_index("y")) * 2 + core_index
    own = lax.dynamic_slice_in_dim(raw_mine, shard * 2, 2, 0)
    sib = lax.dynamic_slice_in_dim(raw_other, shard * 2, 2, 0)
    raw = jnp.where(core_index == 0, jnp.concatenate([own, sib], 1), jnp.concatenate([sib, own], 1))
    new_right = lax.dot_general(raw, inverse, (((1,), (1,)), ((), ())), precision=HIGH, preferred_element_type=F32)
    return new_error, new_momentum, new_params, new_right.reshape(256, 128)


def solution(mesh):
    fine = Mesh(mesh.devices.reshape(4, 4, 4, 2), ("x", "z", "y", "core"))
    shard = ("z", "y", "core")
    return jax.shard_map(
        local,
        mesh=fine,
        in_specs=(P("x", shard, None), P("x", shard, None), P(shard, None), P(shard, None), P(shard, None)),
        out_specs=(P("x", shard, None), P(shard, None), P(shard, None), P(shard, None)),
        check_vma=False,
    )
```

```python
import jax
import jax.numpy as jnp
from jax import lax
from jax.experimental import pallas as pl
from jax.experimental.pallas import tpu as pltpu
from jax.sharding import Mesh, PartitionSpec as P

F32 = jnp.float32
BF16 = jnp.bfloat16
HIGH = lax.Precision.HIGHEST
CHIPS = ("x", "z", "y")
PLANE = ("z", "y")
VMEM = pl.BlockSpec(memory_space=pltpu.VMEM)
SMEM = pl.BlockSpec(memory_space=pltpu.SMEM)


def split(value):
    high = value.astype(BF16)
    return high, (value - high.astype(F32)).astype(BF16)


def dot(a, b):
    return jnp.dot(a, b, preferred_element_type=F32)


def ring(array, axis, step):
    n = lax.axis_size(axis)
    return lax.ppermute(array, axis, [(i, (i + step) % n) for i in range(n)])


def exchange(array, axis):
    return array, ring(array, axis, 2), ring(array, axis, 1), ring(array, axis, -1)


def total(parts):
    return (parts[0] + parts[1]) + (parts[2] + parts[3])


def call(kernel, out_shape, in_specs, out_specs, **kwargs):
    return pl.pallas_call(
        kernel,
        out_shape=out_shape,
        in_specs=in_specs,
        out_specs=out_specs,
        compiler_params=pltpu.CompilerParams(vmem_limit_bytes=24 << 20),
        **kwargs,
    )


def first_half(shape):
    return lax.broadcasted_iota(jnp.int32, shape, len(shape) - 1) < 64


def merge_kernel(where, grad, error, home, *away):
    for step in range(4):
        quarter = lax.rem(where[0] + step, 4)
        odd = lax.rem(quarter, 2)
        for tile in range(16):
            first = pl.multiple_of(tile * 512 + (quarter // 2) * 128, 128)
            low, high = pl.ds(first, 128), pl.ds(first + 256, 128)
            low = grad[0, :, low].astype(F32) + error[0, :, low].astype(F32)
            high = grad[0, :, high].astype(F32) + error[0, :, high].astype(F32)
            joined = jnp.where(
                first_half((128, 128)), pltpu.roll(low, 64 * odd, 1), pltpu.roll(high, 64 * (1 - odd), 1)
            )
            cols = slice(tile * 128, tile * 128 + 128)
            if step == 0:
                home[:, cols] = joined
            else:
                away[2 * step - 2][:, cols] = joined[:64]
                away[2 * step - 1][:, cols] = joined[64:]


def left_kernel(where, home, a0, b0, a1, b1, mine, other, merged, out):
    acc = jnp.zeros((256, 256), F32)
    for pair in range(8):
        cols = slice(pair * 256, pair * 256 + 256)
        came = jnp.concatenate([a0[:, cols] + a1[:, cols], b0[:, cols] + b1[:, cols]], 0)
        value = home[:, cols] + came
        merged[:, cols] = value
        rows = jnp.concatenate(split(value), 0)
        tiles = []
        for tile in (2 * pair, 2 * pair + 1):
            here, there = mine[tile], other[tile]
            tiles += [jnp.where(where[1] == 0, here, there), jnp.where(where[1] == 0, there, here)]
        acc += dot(rows, jnp.concatenate(split(jnp.concatenate(tiles, 0)), 1))
    acc = acc[:128] + acc[128:]
    out[...] = acc[:, :128] + acc[:, 128:]


def raw_tiles(half, parts, merged, left_t, store):
    left = total([part[...] for part in parts]) * 0.25
    left_t[...] = left.T
    high, low = split(left_t[pl.ds(pl.multiple_of(half * 64, 64), 64), :])
    rows = jnp.concatenate(
        [jnp.concatenate([high, high], 1), jnp.concatenate([low, jnp.zeros_like(low)], 1)], 0
    )
    for pair in range(8):
        block = dot(rows, jnp.concatenate(split(merged[:, pair * 256 : pair * 256 + 256]), 0))
        block = block[:64] + block[64:]
        store(2 * pair, block[:, :128])
        store(2 * pair + 1, block[:, 128:])
    return left


def away_kernel(where, p0, p1, p2, p3, merged, out, left_out, gram, left_t):
    def store(index, block):
        out[index] = block

    left = raw_tiles(1 - where[1], (p0, p1, p2, p3), merged, left_t, store)
    left_out[...] = left
    gram[...] = lax.dot(left_t[...], left, precision=HIGH, preferred_element_type=F32)


def home_kernel(where, p0, p1, p2, p3, merged, came, out, left_t):
    def store(index, block):
        out[index] = block + came[index]

    raw_tiles(where[1], (p0, p1, p2, p3), merged, left_t, store)


def sum_kernel(parts, out):
    whole = jnp.sum(parts[...], 0) * 0.25
    for piece in range(out.shape[0]):
        out[piece] = whole


def last_kernel(where, factor, mine, other, grad, error, momentum, params, new_error, new_momentum, new_params):
    weights = factor[...]
    weights = jnp.where(where[1] == 0, weights, pltpu.roll(weights, 64, 1))
    high, low = split(weights)
    rows = jnp.concatenate(
        [jnp.concatenate([high, high], 1), jnp.concatenate([low, jnp.zeros_like(low)], 1)], 0
    )
    lower = first_half((128, 128))
    for tile in range(mine.shape[1]):
        raw = [jnp.concatenate([mine[q, tile], other[q, tile]], 0) for q in range(4)]
        turned = [pltpu.roll(r, 64, 1) for r in raw]
        for run in range(2):
            if run == 0:
                block = [jnp.where(lower, raw[q], turned[q + 1]) for q in (0, 2)]
            else:
                block = [jnp.where(lower, turned[q], raw[q + 1]) for q in (0, 2)]
            approx = dot(rows, jnp.concatenate(split(jnp.concatenate(block, 1)), 0))
            approx = approx[:128] + approx[128:]
            start = tile * 512 + run * 256
            cols = slice(start, start + 256)
            merged = grad[0, :, cols].astype(F32) + error[0, :, cols].astype(F32)
            new_error[0, :, cols] = (merged - approx).astype(BF16)
            moment = 0.9 * momentum[:, cols].astype(F32) + approx
            new_momentum[:, cols] = moment.astype(BF16)
            new_params[:, cols] = params[:, cols] - 0.7 * (approx + 0.9 * moment)


def local(pseudo_grad, error_buf, momentum, params, right_factor):
    x, core = lax.axis_index("x"), lax.axis_index("core")
    plane = lax.axis_index("z") * 4 + lax.axis_index("y")
    where = jnp.stack([x, core]).astype(jnp.int32)
    square = jax.ShapeDtypeStruct((128, 128), F32)
    quarter = jax.ShapeDtypeStruct((128, 2048), F32)
    half = jax.ShapeDtypeStruct((64, 2048), F32)
    tiles = jax.ShapeDtypeStruct((16, 64, 128), F32)

    home, a1, b1, a2, b2, a3, b3 = call(merge_kernel, (quarter,) + (half,) * 6, [SMEM, VMEM, VMEM], (VMEM,) * 7)(
        where, pseudo_grad, error_buf
    )
    far_a, far_b = ring(a2, "x", 1), ring(b2, "x", -1)
    b_right, a_left = ring(b1, "x", 1), ring(a3, "x", -1)
    a_right, b_left = ring(a1 + far_a, "x", 1), ring(b3 + far_b, "x", -1)

    rows = lax.dynamic_slice_in_dim(right_factor, x * 64, 64, 0)
    mine = lax.all_to_all(jnp.broadcast_to(rows[None], (16, 64, 128)), PLANE, 0, 0)
    other = ring(mine, "core", 1)

    merged, part = call(left_kernel, (quarter, square), [SMEM] + [VMEM] * 7, (VMEM,) * 2)(
        where, home, a_right, b_right, a_left, b_left, mine, other
    )
    parts = exchange(part, "x")
    scratch = [pltpu.VMEM((128, 128), F32)]
    away, left, gram = call(
        away_kernel, (tiles, square, square), [SMEM] + [VMEM] * 5, (VMEM,) * 3, scratch_shapes=scratch
    )(where, *parts, merged)
    came = ring(away, "core", 1)
    raw = call(home_kernel, tiles, [SMEM] + [VMEM] * 6, VMEM, scratch_shapes=scratch)(where, *parts, merged, came)
    shares = lax.all_to_all(raw, PLANE, 0, 0)
    copies = call(sum_kernel, jax.ShapeDtypeStruct((64, 64, 128), F32), [VMEM], VMEM)(shares)
    raw_mine = lax.all_to_all(copies, CHIPS, 0, 0).reshape(4, 16, 64, 128)

    gram = gram + ring(gram, "core", 1)
    gram = total(exchange(gram, "y"))
    gram = total(exchange(gram, "z"))
    eye = jnp.eye(128, dtype=F32)
    gram = gram + 1e-06 * jnp.trace(gram) / 128 * eye
    lower = jnp.linalg.cholesky(gram)
    inverse = lax.linalg.triangular_solve(lower, eye, left_side=True, lower=True)
    factor = jnp.dot(jnp.dot(left, inverse.T, precision=HIGH), inverse, precision=HIGH)

    raw_mine, factor, inverse = lax.optimization_barrier((raw_mine, factor, inverse))
    raw_other = ring(raw_mine, "core", 1)

    n = 8
    wide = 8192 // n
    strip3 = pl.BlockSpec((1, 128, wide), lambda i: (0, 0, i))
    strip = pl.BlockSpec((128, wide), lambda i: (0, i))
    raw_spec = pl.BlockSpec((4, 16 // n, 64, 128), lambda i: (0, i, 0, 0))
    whole = pl.BlockSpec((128, 128), lambda i: (0, 0))
    new_error, new_momentum, new_params = call(
        last_kernel,
        (
            jax.ShapeDtypeStruct(error_buf.shape, BF16),
            jax.ShapeDtypeStruct(momentum.shape, BF16),
            jax.ShapeDtypeStruct(params.shape, F32),
        ),
        [SMEM, whole, raw_spec, raw_spec, strip3, strip3, strip, strip],
        (strip3, strip, strip),
        grid=(n,),
    )(where, factor, raw_mine, raw_other, pseudo_grad, error_buf, momentum, params)

    own = lax.dynamic_slice(raw_mine, (0, plane, 0, core * 64), (4, 1, 64, 64))[:, 0]
    sib = lax.dynamic_slice(raw_other, (0, plane, 0, core * 64), (4, 1, 64, 64))[:, 0]
    raw = jnp.where(core == 0, jnp.concatenate([own, sib], 1), jnp.concatenate([sib, own], 1))
    new_right = lax.dot_general(raw, inverse, (((1,), (1,)), ((), ())), precision=HIGH, preferred_element_type=F32)
    return new_error, new_momentum, new_params, new_right.reshape(256, 128)


def solution(mesh):
    fine = Mesh(mesh.devices.reshape(4, 4, 4, 2), ("x", "z", "y", "core"))
    shard = ("z", "y", "core")
    return jax.shard_map(
        local,
        mesh=fine,
        in_specs=(P("x", shard, None), P("x", shard, None), P(shard, None), P(shard, None), P(shard, None)),
        out_specs=(P("x", shard, None), P(shard, None), P(shard, None), P(shard, None)),
        check_vma=False,
    )
```

```python
import jax
import jax.numpy as jnp
from jax import lax
from jax.experimental import pallas as pl
from jax.experimental.pallas import tpu as pltpu
from jax.sharding import Mesh, PartitionSpec as P

F32 = jnp.float32
BF16 = jnp.bfloat16
HIGH = lax.Precision.HIGHEST
CHIPS = ("z", "y", "x")
PLANE = ("z", "y")
VMEM = pl.BlockSpec(memory_space=pltpu.VMEM)
HBM = pl.BlockSpec(memory_space=pltpu.HBM)
SMEM = pl.BlockSpec(memory_space=pltpu.SMEM)


def split(value):
    high = value.astype(BF16)
    return high, (value - high.astype(F32)).astype(BF16)


def dot(a, b):
    return jnp.dot(a, b, preferred_element_type=F32)


def ring(array, axis, step):
    n = lax.axis_size(axis)
    return lax.ppermute(array, axis, [(i, (i + step) % n) for i in range(n)])


def exchange(array, axis):
    return array, ring(array, axis, 2), ring(array, axis, 1), ring(array, axis, -1)


def total(parts):
    return (parts[0] + parts[1]) + (parts[2] + parts[3])


def call(kernel, out_shape, in_specs, out_specs, **kwargs):
    return pl.pallas_call(
        kernel,
        out_shape=out_shape,
        in_specs=in_specs,
        out_specs=out_specs,
        compiler_params=pltpu.CompilerParams(vmem_limit_bytes=12 << 20),
        **kwargs,
    )


def first_half(shape):
    return lax.broadcasted_iota(jnp.int32, shape, len(shape) - 1) < 64


def quarter_tile(quarter, tile, grad, error):
    odd = lax.rem(quarter, 2)
    first = pl.multiple_of(tile * 512 + (quarter // 2) * 128, 128)
    low, high = pl.ds(first, 128), pl.ds(first + 256, 128)
    low = grad[0, :, low].astype(F32) + error[0, :, low].astype(F32)
    high = grad[0, :, high].astype(F32) + error[0, :, high].astype(F32)
    return jnp.where(first_half((128, 128)), pltpu.roll(low, 64 * odd, 1), pltpu.roll(high, 64 * (1 - odd), 1))


def far_kernel(where, grad_in, error_in, grad, error, a2, b2, sems):
    copies = []
    for piece in range(4):
        cols = slice(piece * 2048, piece * 2048 + 2048)
        for k, (source, target) in enumerate(((grad_in, grad), (error_in, error))):
            copy = pltpu.make_async_copy(source.at[:, :, cols], target.at[:, :, cols], sems.at[k, piece])
            copy.start()
            copies.append(copy)
    quarter = lax.rem(where[0] + 2, 4)
    for tile in range(16):
        if tile % 4 == 0:
            copies[tile // 2].wait()
            copies[tile // 2 + 1].wait()
        joined = quarter_tile(quarter, tile, grad, error)
        cols = slice(tile * 128, tile * 128 + 128)
        a2[:, cols] = joined[:64]
        b2[:, cols] = joined[64:]


def near_kernel(where, grad, error, momentum_in, params_in, home, a1, b1, a3, b3, momentum, params, sems):
    copies = [
        pltpu.make_async_copy(momentum_in, momentum, sems.at[0]),
        pltpu.make_async_copy(params_in.at[:64], params.at[:64], sems.at[1]),
        pltpu.make_async_copy(params_in.at[64:], params.at[64:], sems.at[2]),
    ]
    for copy in copies:
        copy.start()
    for tile in range(16):
        cols = slice(tile * 128, tile * 128 + 128)
        home[:, cols] = quarter_tile(where[0], tile, grad, error)
        for step, a, b in ((1, a1, b1), (3, a3, b3)):
            joined = quarter_tile(lax.rem(where[0] + step, 4), tile, grad, error)
            a[:, cols] = joined[:64]
            b[:, cols] = joined[64:]
    for copy in copies:
        copy.wait()


def left_kernel(where, home, a0, b0, a1, b1, mine, other, merged, out):
    acc = jnp.zeros((256, 256), F32)
    for pair in range(8):
        cols = slice(pair * 256, pair * 256 + 256)
        came = jnp.concatenate([a0[:, cols] + a1[:, cols], b0[:, cols] + b1[:, cols]], 0)
        value = home[:, cols] + came
        merged[:, cols] = value
        rows = jnp.concatenate(split(value), 0)
        tiles = []
        for tile in (2 * pair, 2 * pair + 1):
            here, there = mine[tile], other[tile]
            tiles += [jnp.where(where[1] == 0, here, there), jnp.where(where[1] == 0, there, here)]
        acc += dot(rows, jnp.concatenate(split(jnp.concatenate(tiles, 0)), 1))
    acc = acc[:128] + acc[128:]
    out[...] = acc[:, :128] + acc[:, 128:]


def stacked(matrix):
    high, low = split(matrix)
    return jnp.concatenate(
        [jnp.concatenate([high, high], 1), jnp.concatenate([low, jnp.zeros_like(low)], 1)], 0
    )


def raw_kernel(where, p0, p1, p2, p3, merged, own, away, left_out):
    left = total([p0[...], p1[...], p2[...], p3[...]]) * 0.25
    left_out[...] = left
    turned = left.T
    turned = jnp.where(where[1] == 0, turned, jnp.concatenate([turned[64:], turned[:64]], 0))
    rows = stacked(turned)
    for pair in range(8):
        block = dot(rows, jnp.concatenate(split(merged[:, pair * 256 : pair * 256 + 256]), 0))
        block = block[:128] + block[128:]
        for k in range(2):
            own[2 * pair + k] = block[:64, k * 128 : k * 128 + 128]
            away[2 * pair + k] = block[64:, k * 128 : k * 128 + 128]
    gram = lax.dot(turned, left, precision=HIGH, preferred_element_type=F32)
    own[16] = gram[:64]
    away[16] = gram[64:]


def pack_kernel(own, came, out):
    gram = own[16] + came[16]
    for tile in range(16):
        out[tile, :64] = own[tile] + came[tile]
        out[tile, 64:] = gram


def sum_kernel(parts, out, gram, block, sems):
    whole = parts[0]
    for piece in range(1, 16):
        whole += parts[piece]
    gram[...] = whole[64:]
    whole = whole[:64] * 0.25
    for piece in range(8):
        block[piece] = whole
    copies = [pltpu.make_async_copy(block, out.at[pl.ds(8 * piece, 8)], sems.at[piece]) for piece in range(8)]
    for copy in copies:
        copy.start()
    for copy in copies:
        copy.wait()


def pair_up(raw, quarters, second):
    lower = first_half((128, 128))
    first, last = (raw[q] for q in quarters)
    if second:
        return jnp.where(lower, pltpu.roll(first, 64, 1), last)
    return jnp.where(lower, first, pltpu.roll(last, 64, 1))


def outer_step(base, where, factor, mine, other, grad, error, momentum, params, outs, stages, sems):
    weights = factor[...]
    weights = jnp.where(where[1] == 0, weights, pltpu.roll(weights, 64, 1))
    rows = stacked(weights)
    copies = []
    for tile in range(8):
        raw = [jnp.concatenate([mine[base + tile, q], other[tile, q]], 0) for q in range(4)]
        for run in range(2):
            block = [pair_up(raw, (0, 1), run == 1), pair_up(raw, (2, 3), run == 1)]
            approx = dot(rows, jnp.concatenate(split(jnp.concatenate(block, 1)), 0))
            approx = approx[:128] + approx[128:]
            start = tile * 512 + run * 256
            cols, there = slice(start, start + 256), slice(base * 512 + start, base * 512 + start + 256)
            merged = grad[0, :, there].astype(F32) + error[0, :, there].astype(F32)
            stages[0][0, :, cols] = (merged - approx).astype(BF16)
            moment = 0.9 * momentum[:, there].astype(F32) + approx
            stages[1][:, cols] = moment.astype(BF16)
            stages[2][:, cols] = params[:, there] - 0.7 * (approx + 0.9 * moment)
        if tile % 2 == 1:
            cols = slice((tile - 1) * 512, (tile + 1) * 512)
            there = slice((base + tile - 1) * 512, (base + tile + 1) * 512)
            for k in range(3):
                lead = (slice(None),) * (2 if k == 0 else 1)
                copy = pltpu.make_async_copy(
                    stages[k].at[lead + (cols,)], outs[k].at[lead + (there,)], sems.at[k, tile // 2]
                )
                copy.start()
                copies.append(copy)
    return copies


def lower_kernel(where, factor, mine, other, grad, error, momentum, params, o0, o1, o2, s0, s1, s2, sems):
    for copy in outer_step(0, where, factor, mine, other, grad, error, momentum, params, (o0, o1, o2), (s0, s1, s2), sems):
        copy.wait()


def upper_kernel(
    where, factor, inverse, mine, low, other, grad, error, momentum, params, i0, i1, i2, o0, o1, o2, right, s0, s1, s2, sems
):
    copies = outer_step(8, where, factor, mine, other, grad, error, momentum, params, (o0, o1, o2), (s0, s1, s2), sems)
    place = where[2]
    sibling = jnp.where(place < 8, low[lax.rem(place, 8)], other[lax.rem(place, 8)])
    here = mine[place]
    first = where[1] == 0
    raw = [
        jnp.concatenate([jnp.where(first, here[q], sibling[q]), jnp.where(first, sibling[q], here[q])], 0)
        for q in range(4)
    ]
    for k in range(2):
        block = jnp.where(
            first, pair_up(raw, (2 * k, 2 * k + 1), False), pair_up(raw, (2 * k, 2 * k + 1), True)
        )
        block = lax.dot(inverse[...], block, precision=HIGH, preferred_element_type=F32)
        right[k * 128 : k * 128 + 128, :] = block.T
    for copy in copies:
        copy.wait()


def local(pseudo_grad, error_buf, momentum, params, right_factor):
    x, core = lax.axis_index("x"), lax.axis_index("core")
    plane = lax.axis_index("z") * 4 + lax.axis_index("y")
    where = jnp.stack([x, core, plane]).astype(jnp.int32)
    square = jax.ShapeDtypeStruct((128, 128), F32)
    wide = (64, 2048)

    grad, error, a2, b2 = call(
        far_kernel,
        (pltpu.VMEM(pseudo_grad.shape, BF16), pltpu.VMEM(error_buf.shape, BF16), pltpu.VMEM(wide, F32), pltpu.VMEM(wide, F32)),
        [SMEM, HBM, HBM],
        (VMEM,) * 4,
        scratch_shapes=[pltpu.SemaphoreType.DMA((2, 4))],
    )(where, pseudo_grad, error_buf)
    far_a, far_b = ring(a2, "x", 1), ring(b2, "x", -1)
    home, a1, b1, a3, b3, momentum, params = call(
        near_kernel,
        (pltpu.VMEM((128, 2048), F32),)
        + (pltpu.VMEM(wide, F32),) * 4
        + (pltpu.VMEM(momentum.shape, BF16), pltpu.VMEM(params.shape, F32)),
        [SMEM, VMEM, VMEM, HBM, HBM],
        (VMEM,) * 7,
        scratch_shapes=[pltpu.SemaphoreType.DMA((3,))],
    )(where, grad, error, momentum, params)
    b_right, a_left = ring(b1, "x", 1), ring(a3, "x", -1)
    a_right, b_left = ring(a1 + far_a, "x", 1), ring(b3 + far_b, "x", -1)

    rows = lax.dynamic_slice_in_dim(right_factor, x * 64, 64, 0)
    mine = lax.all_to_all(jnp.broadcast_to(rows[None], (16, 64, 128)), PLANE, 0, 0)
    other = ring(mine, "core", 1)

    merged, part = call(left_kernel, (pltpu.VMEM((128, 2048), F32), square), [SMEM] + [VMEM] * 7, (VMEM,) * 2)(
        where, home, a_right, b_right, a_left, b_left, mine, other
    )
    parts = exchange(part, "x")
    seventeen = pltpu.VMEM((17, 64, 128), F32)
    own, away, left = call(raw_kernel, (seventeen, seventeen, square), [SMEM] + [VMEM] * 5, (VMEM,) * 3)(
        where, *parts, merged
    )
    came = ring(away, "core", 1)
    raw = call(pack_kernel, jax.ShapeDtypeStruct((16, 128, 128), F32), [VMEM] * 2, VMEM)(own, came)
    shares = lax.all_to_all(raw, PLANE, 0, 0)
    copies, gram = call(
        sum_kernel,
        (pltpu.HBM((64, 64, 128), F32), jax.ShapeDtypeStruct((64, 128), F32)),
        [VMEM],
        (HBM, VMEM),
        scratch_shapes=[pltpu.VMEM((8, 64, 128), F32), pltpu.SemaphoreType.DMA((8,))],
    )(shares)
    raw_mine = lax.all_to_all(copies, CHIPS, 0, 0).reshape(16, 4, 64, 128)

    gram_other = ring(gram, "core", 1)
    gram = jnp.where(core == 0, jnp.concatenate([gram, gram_other], 0), jnp.concatenate([gram_other, gram], 0))
    eye = jnp.eye(128, dtype=F32)
    gram = gram + 1e-06 * jnp.trace(gram) / 128 * eye
    lower = jnp.linalg.cholesky(gram)
    inverse = lax.linalg.triangular_solve(lower, eye, left_side=True, lower=True)
    factor = jnp.dot(jnp.dot(left, inverse.T, precision=HIGH), inverse, precision=HIGH)

    raw_mine, factor, inverse = lax.optimization_barrier((raw_mine, factor, inverse))
    low = ring(raw_mine[:8], "core", 1)
    high = ring(raw_mine[8:], "core", 1)

    outs = (pltpu.HBM(error_buf.shape, BF16), pltpu.HBM(momentum.shape, BF16), pltpu.HBM(params.shape, F32))
    scratch = [
        pltpu.VMEM((1, 128, 4096), BF16),
        pltpu.VMEM((128, 4096), BF16),
        pltpu.VMEM((128, 4096), F32),
        pltpu.SemaphoreType.DMA((3, 4)),
    ]
    begun = call(lower_kernel, outs, [SMEM] + [VMEM] * 7, (HBM,) * 3, scratch_shapes=scratch)(
        where, factor, raw_mine, low, grad, error, momentum, params
    )
    return call(
        upper_kernel,
        outs + (jax.ShapeDtypeStruct((256, 128), F32),),
        [SMEM] + [VMEM] * 9 + [HBM] * 3,
        (HBM,) * 3 + (VMEM,),
        scratch_shapes=scratch,
        input_output_aliases={10: 0, 11: 1, 12: 2},
    )(where, factor, inverse, raw_mine, low, high, grad, error, momentum, params, *begun)


def solution(mesh):
    fine = Mesh(mesh.devices.reshape(4, 4, 4, 2), ("x", "z", "y", "core"))
    shard = ("z", "y", "core")
    return jax.shard_map(
        local,
        mesh=fine,
        in_specs=(P("x", shard, None), P("x", shard, None), P(shard, None), P(shard, None), P(shard, None)),
        out_specs=(P("x", shard, None), P(shard, None), P(shard, None), P(shard, None)),
        check_vma=False,
    )
```

```python
import functools

import jax
import jax.numpy as jnp
from jax import lax
from jax.experimental import pallas as pl
from jax.experimental.pallas import tpu as pltpu
from jax.sharding import Mesh, PartitionSpec as P

F32 = jnp.float32
BF16 = jnp.bfloat16
HIGH = lax.Precision.HIGHEST
PLANE = ("z", "y")
GRANT = 58
VMEM = pl.BlockSpec(memory_space=pltpu.VMEM)
ANY = pl.BlockSpec(memory_space=pl.ANY)


def split(value):
    high = value.astype(BF16)
    return high, (value - high.astype(F32)).astype(BF16)


def dot(a, b):
    return jnp.dot(a, b, preferred_element_type=F32)


def ring(array, axis, step):
    n = lax.axis_size(axis)
    return lax.ppermute(array, axis, [(i, (i + step) % n) for i in range(n)])


def exchange(array, axis):
    return array, ring(array, axis, 2), ring(array, axis, 1), ring(array, axis, -1)


def total(parts):
    return (parts[0] + parts[1]) + (parts[2] + parts[3])


def call(kernel, out_shape, in_specs, out_specs, us, grant=12, **kwargs):
    return pl.pallas_call(
        kernel,
        out_shape=out_shape,
        in_specs=in_specs,
        out_specs=out_specs,
        cost_estimate=pl.CostEstimate(flops=int(us * 1.1e9), bytes_accessed=1 << 20, transcendentals=0),
        compiler_params=pltpu.CompilerParams(vmem_limit_bytes=grant << 20),
        **kwargs,
    )


def begin(source, target, sem):
    copy = pltpu.make_async_copy(source, target, sem)
    copy.start()
    return copy


def hdot(a, b, contract):
    return lax.dot_general(a, b, (contract, ((), ())), precision=HIGH, preferred_element_type=F32)


def first_half(shape):
    return lax.broadcasted_iota(jnp.int32, shape, len(shape) - 1) < 64


def columns(ref, start, size):
    lead = (slice(None),) * (len(ref.shape) - 1)
    return ref.at[lead + (slice(start, start + size),)]


def quarter_tile(quarter, tile, rows, grad, error):
    odd = lax.rem(quarter, 2)
    first = pl.multiple_of(tile * 512 + (quarter // 2) * 128, 128)
    low, high = pl.ds(first, 128), pl.ds(first + 256, 128)
    low = grad[0, rows, low].astype(F32) + error[0, rows, low].astype(F32)
    high = grad[0, rows, high].astype(F32) + error[0, rows, high].astype(F32)
    return jnp.where(first_half(low.shape), pltpu.roll(low, 64 * odd, 1), pltpu.roll(high, 64 * (1 - odd), 1))


def quarters_kernel(jobs, sizes, grad_in, error_in, *rest):
    count = len(sizes)
    outs, (grad, error), stages = rest[:count], rest[count : count + 2], rest[count + 2 : -2]
    in_sems, out_sems = rest[-2:]
    arrive = []
    for piece in range(4):
        arrive.append(begin(columns(grad_in, piece * 2048, 2048), columns(grad, piece * 2048, 2048), in_sems.at[0, piece]))
        arrive.append(begin(columns(error_in, piece * 2048, 2048), columns(error, piece * 2048, 2048), in_sems.at[1, piece]))
    leave = []
    for piece in range(4):
        arrive[2 * piece].wait()
        arrive[2 * piece + 1].wait()
        for tile in range(4 * piece, 4 * piece + 4):
            cols = slice(tile * 128, tile * 128 + 128)
            for step, start, stop, out, at in jobs:
                quarter = lax.rem(lax.axis_index("x") + step, 4)
                stages[out][at : at + stop - start, cols] = quarter_tile(quarter, tile, slice(start, stop), grad, error)
        for k in range(count):
            source, target = (columns(ref[k], piece * 512, 512) for ref in (stages, outs))
            leave.append(begin(source, target, out_sems.at[k, piece]))
    for copy in leave:
        copy.wait()


def add_kernel(right, left, a, b, upper, lower):
    upper[...] = a[...] + right[:64]
    lower[...] = b[...] + left[:64]


def left_kernel(home, right, left, upper, lower, mine, other, merged, out):
    first = lax.axis_index("core") == 0
    acc = jnp.zeros((256, 256), F32)
    for pair in range(8):
        cols = slice(pair * 256, pair * 256 + 256)
        here = jnp.concatenate([upper[:, cols], lower[:, cols]], 0)
        came = jnp.concatenate([left[64:, cols], right[64:, cols]], 0)
        value = home[:, cols] + here + came
        merged[:, cols] = value
        rows = jnp.concatenate(split(value), 0)
        tiles = []
        for tile in (2 * pair, 2 * pair + 1):
            here, there = mine[tile], other[tile]
            tiles += [jnp.where(first, here, there), jnp.where(first, there, here)]
        acc += dot(rows, jnp.concatenate(split(jnp.concatenate(tiles, 0)), 1))
    acc = acc[:128] + acc[128:]
    out[...] = acc[:, :128] + acc[:, 128:]


def stacked(matrix):
    high, low = split(matrix)
    return jnp.concatenate(
        [jnp.concatenate([high, high], 1), jnp.concatenate([low, jnp.zeros_like(low)], 1)], 0
    )


def raw_kernel(p0, p1, p2, p3, merged, own, away, left_out):
    left = total([p0[...], p1[...], p2[...], p3[...]]) * 0.25
    left_out[...] = left
    turned = left.T
    turned = jnp.where(lax.axis_index("core") == 0, turned, jnp.concatenate([turned[64:], turned[:64]], 0))
    rows = stacked(turned)
    gram = lax.dot(turned, left, precision=HIGH, preferred_element_type=F32)
    for step in range(4):
        y = lax.rem(lax.axis_index("y") + step, 4)
        for pair in range(2):
            cols = [pl.ds(pl.multiple_of((4 * z + y) * 128, 128), 128) for z in (2 * pair, 2 * pair + 1)]
            block = jnp.concatenate([merged[:, c] for c in cols], 1)
            block = dot(rows, jnp.concatenate(split(block), 0))
            block = block[:128] + block[128:]
            for k in range(2):
                own[step * 5 + 2 * pair + k] = block[:64, k * 128 : k * 128 + 128]
                away[step * 5 + 2 * pair + k] = block[64:, k * 128 : k * 128 + 128]
        own[step * 5 + 4] = gram[:64]
        away[step * 5 + 4] = gram[64:]


def pack_kernel(own, came, *outs):
    for step in range(4):
        outs[step][...] = own[5 * step : 5 * step + 5] + came[5 * step : 5 * step + 5]


def sum_kernel(p0, p1, p2, p3, out):
    out[...] = total([p0[...], p1[...], p2[...], p3[...]])


def split_kernel(p0, p1, p2, p3, tiles, gram):
    whole = total([p0[...], p1[...], p2[...], p3[...]])
    tiles[...] = whole[:4] * 0.25
    gram[...] = whole[4]


def gather_kernel(p0, p1, p2, p3, out):
    for part, step in ((p0, 0), (p1, 2), (p2, 3), (p3, 1)):
        y = lax.rem(lax.axis_index("y") + step, 4)
        for z in range(4):
            out[4 * z + y] = part[z]


def pair_up(raw, quarters, second):
    lower = first_half((128, 128))
    first, last = (raw[q] for q in quarters)
    if second:
        return jnp.where(lower, pltpu.roll(first, 64, 1), last)
    return jnp.where(lower, first, pltpu.roll(last, 64, 1))


def eliminate(work, starts, size=32):
    below = lax.broadcasted_iota(jnp.int32, (size, 1), 0)
    lane = lax.broadcasted_iota(jnp.int32, (size, 128), 1)
    for start in starts:
        stop = start + size
        panel = work[start:stop, :]
        scales = []
        for j in range(size):
            scale = 1.0 / panel[j : j + 1, start + j : start + j + 1]
            column = jnp.where(below > j, panel[:, start + j : start + j + 1] * scale, 0.0)
            panel = panel - column * panel[j : j + 1, :]
            scales.append(scale)
        scale = jnp.concatenate(scales, 0)
        work[start:stop, :] = panel * lax.sqrt(scale)
        if stop < 128:
            steps = jnp.where(lane >= stop, panel[:, :128] * scale, 0.0)
            work[stop:, :] = work[stop:, :] - hdot(steps, panel, ((0,), (0,)))[stop:]


def begin_factor_kernel(gram, came, work):
    first = lax.axis_index("core") == 0
    gram, came = gram[...], came[...]
    gram = jnp.concatenate([jnp.where(first, gram, came), jnp.where(first, came, gram)], 0)
    row = lax.broadcasted_iota(jnp.int32, (128, 128), 0)
    diagonal = row == lax.broadcasted_iota(jnp.int32, (128, 128), 1)
    eye = jnp.where(diagonal, 1.0, 0.0)
    trace = jnp.sum(jnp.where(diagonal, gram, 0.0))
    work[:, :128] = gram + 1e-06 * trace / 128 * eye
    work[:, 128:] = eye
    eliminate(work, (0,))


def end_factor_kernel(begun, left, factor, inverse, work):
    work[...] = begun[...]
    eliminate(work, (32, 64, 96))
    lower = work[:, 128:]
    inverse[...] = lower
    factor[...] = hdot(hdot(left[...], lower, ((1,), (1,))), lower, ((1,), (0,)))


def last_kernel(factor, inverse, *rest):
    raws, (grad, error, momentum, params), outs, right = rest[:10], rest[10:14], rest[14:17], rest[17]
    here, stages, in_sems, out_sems = rest[18], rest[19:22], rest[22], rest[23]
    x, place = lax.axis_index("x"), lax.axis_index("z") * 4 + lax.axis_index("y")
    arrive = ([], [])
    for part in range(2):
        for half in range(2):
            for k, step in enumerate((0, 1, 3, 2)):
                source = raws[5 * half + k].at[slice(8 * part, 8 * part + 8)] if k < 3 else raws[5 * half + 3 + part]
                target = here.at[half, lax.rem(x + step, 4), slice(8 * part, 8 * part + 8)]
                arrive[part].append(begin(source, target, in_sems.at[part, 4 * half + k]))
    first = lax.axis_index("core") == 0
    weights = factor[...]
    rows = stacked(jnp.where(first, weights, pltpu.roll(weights, 64, 1)))
    leave = []
    for tile in range(16):
        if tile % 8 == 0:
            for copy in arrive[tile // 8]:
                copy.wait()
        raw = [jnp.concatenate([here[0, q, tile], here[1, q, tile]], 0) for q in range(4)]
        for run in range(2):
            block = [pair_up(raw, (0, 1), run == 1), pair_up(raw, (2, 3), run == 1)]
            approx = dot(rows, jnp.concatenate(split(jnp.concatenate(block, 1)), 0))
            approx = approx[:128] + approx[128:]
            cols = slice(tile * 512 + run * 256, tile * 512 + run * 256 + 256)
            merged = grad[0, :, cols].astype(F32) + error[0, :, cols].astype(F32)
            stages[0][0, :, cols] = (merged - approx).astype(BF16)
            moment = 0.9 * momentum[:, cols].astype(F32) + approx
            stages[1][:, cols] = moment.astype(BF16)
            stages[2][:, cols] = params[:, cols] - 0.7 * (approx + 0.9 * moment)
        if tile % 2 == 1:
            for k in range(3):
                source, target = (columns(ref[k], (tile - 1) * 512, 1024) for ref in (stages, outs))
                leave.append(begin(source, target, out_sems.at[k, tile // 2]))
    raw = [
        jnp.concatenate(
            [
                jnp.where(first, here[0, q, place], here[1, q, place]),
                jnp.where(first, here[1, q, place], here[0, q, place]),
            ],
            0,
        )
        for q in range(4)
    ]
    for k in range(2):
        block = jnp.where(
            first, pair_up(raw, (2 * k, 2 * k + 1), False), pair_up(raw, (2 * k, 2 * k + 1), True)
        )
        block = hdot(inverse[...], block, ((1,), (0,)))
        right[k * 128 : k * 128 + 128, :] = block.T
    for copy in leave:
        copy.wait()


def quarters(jobs, sizes, grad, error):
    shapes = [(size, 2048) for size in sizes]
    return call(
        functools.partial(quarters_kernel, jobs, sizes),
        tuple(jax.ShapeDtypeStruct(shape, F32) for shape in shapes),
        [ANY, ANY],
        (ANY,) * len(shapes),
        us=4,
        grant=GRANT,
        scratch_shapes=[pltpu.VMEM((1, 128, 8192), BF16)] * 2
        + [pltpu.VMEM(shape, F32) for shape in shapes]
        + [pltpu.SemaphoreType.DMA((2, 4)), pltpu.SemaphoreType.DMA((len(shapes), 4))],
    )(grad, error)


def local(grad, error, momentum, params, right_factor):
    x = lax.axis_index("x")
    square = jax.ShapeDtypeStruct((128, 128), F32)
    tiles = lambda n: jax.ShapeDtypeStruct((n, 64, 128), F32)

    right, left = quarters(
        ((2, 0, 64, 0, 0), (1, 64, 128, 0, 64), (2, 64, 128, 1, 0), (3, 0, 64, 1, 64)), (128, 128), grad, error
    )
    right, left = ring(right, "x", 1), ring(left, "x", -1)
    home, a1, b3 = quarters(((0, 0, 128, 0, 0), (1, 0, 64, 1, 0), (3, 64, 128, 2, 0)), (128, 64, 64), grad, error)
    rows = lax.dynamic_slice_in_dim(right_factor, x * 64, 64, 0)
    mine = lax.all_to_all(jnp.broadcast_to(rows[None], (16, 64, 128)), PLANE, 0, 0)
    right, left, home, a1, b3, mine = lax.optimization_barrier((right, left, home, a1, b3, mine))
    half = jax.ShapeDtypeStruct((64, 2048), F32)
    a1, b3 = call(add_kernel, (half, half), [VMEM] * 4, (VMEM,) * 2, us=0.6)(right, left, a1, b3)
    a_right, b_left = ring(a1, "x", 1), ring(b3, "x", -1)
    other = ring(mine, "core", 1)

    merged, part = call(
        left_kernel, (jax.ShapeDtypeStruct((128, 2048), F32), square), [VMEM] * 7, (VMEM,) * 2, us=1.2
    )(home, right, left, a_right, b_left, mine, other)
    parts = exchange(part, "x")
    own, away, left_factor = call(raw_kernel, (tiles(20), tiles(20), square), [VMEM] * 5, (VMEM,) * 3, us=1)(*parts, merged)
    came = ring(away, "core", 1)

    outs = call(pack_kernel, (tiles(5),) * 4, [VMEM] * 2, (VMEM,) * 4, us=0.3)(own, came)
    outs = (outs[0], ring(outs[2], "y", 2), ring(outs[1], "y", 1), ring(outs[3], "y", -1))
    part = call(sum_kernel, tiles(5), [VMEM] * 4, VMEM, us=0.2)(*outs)
    mine, gram = call(split_kernel, (tiles(4), jax.ShapeDtypeStruct((64, 128), F32)), [VMEM] * 4, (VMEM,) * 2, us=0.2)(
        *exchange(part, "z")
    )

    gram_other = ring(gram, "core", 1)
    parts = exchange(mine, "y")
    work = call(begin_factor_kernel, jax.ShapeDtypeStruct((128, 256), F32), [VMEM] * 2, VMEM, us=3.4)(gram, gram_other)
    *parts, work = lax.optimization_barrier((*parts, work))
    own = call(gather_kernel, tiles(16), [VMEM] * 4, VMEM, us=0.3)(*parts)
    before, after = ring(own, "x", 1), ring(own, "x", -1)
    own, work = lax.optimization_barrier((own, work))
    factor, inverse = call(
        end_factor_kernel, (square, square), [VMEM] * 2, (VMEM,) * 2, us=9.5, scratch_shapes=[pltpu.VMEM((128, 256), F32)]
    )(work, left_factor)
    before, after, factor, inverse = lax.optimization_barrier((before, after, factor, inverse))
    low, high = ring(before[:8], "x", 1), ring(after[8:], "x", -1)
    raws = (own, after, before, low, high)
    siblings = tuple(ring(array, "core", 1) for array in raws)

    return call(
        last_kernel,
        tuple(jax.ShapeDtypeStruct(array.shape, array.dtype) for array in (error, momentum, params))
        + (jax.ShapeDtypeStruct((256, 128), F32),),
        [VMEM] * 2 + [ANY] * 10 + [VMEM] * 4,
        (ANY,) * 3 + (VMEM,),
        us=7,
        grant=20,
        scratch_shapes=[
            pltpu.VMEM((2, 4, 16, 64, 128), F32),
            pltpu.VMEM((1, 128, 8192), BF16),
            pltpu.VMEM((128, 8192), BF16),
            pltpu.VMEM((128, 8192), F32),
            pltpu.SemaphoreType.DMA((2, 8)),
            pltpu.SemaphoreType.DMA((3, 8)),
        ],
    )(factor, inverse, *raws, *siblings, grad, error, momentum, params)


def solution(mesh):
    fine = Mesh(mesh.devices.reshape(4, 4, 4, 2), ("x", "z", "y", "core"))
    shard = ("z", "y", "core")
    return jax.shard_map(
        local,
        mesh=fine,
        in_specs=(P("x", shard, None), P("x", shard, None), P(shard, None), P(shard, None), P(shard, None)),
        out_specs=(P("x", shard, None), P(shard, None), P(shard, None), P(shard, None)),
        check_vma=False,
    )
```

```python
import functools

import jax
import jax.numpy as jnp
from jax import lax
from jax.experimental import pallas as pl
from jax.experimental.pallas import tpu as pltpu
from jax.sharding import Mesh, PartitionSpec as P

F32 = jnp.float32
BF16 = jnp.bfloat16
HIGH = lax.Precision.HIGHEST
PLANE = ("z", "y")
GRANT = 58
VMEM = pl.BlockSpec(memory_space=pltpu.VMEM)
ANY = pl.BlockSpec(memory_space=pl.ANY)


def split(value):
    high = value.astype(BF16)
    return high, (value - high.astype(F32)).astype(BF16)


def dot(a, b):
    return jnp.dot(a, b, preferred_element_type=F32)


def ring(array, axis, step):
    n = lax.axis_size(axis)
    return lax.ppermute(array, axis, [(i, (i + step) % n) for i in range(n)])


def exchange(array, axis):
    return array, ring(array, axis, 2), ring(array, axis, 1), ring(array, axis, -1)


def total(parts):
    return (parts[0] + parts[1]) + (parts[2] + parts[3])


def call(kernel, out_shape, in_specs, out_specs, us, grant=12, **kwargs):
    return pl.pallas_call(
        kernel,
        out_shape=out_shape,
        in_specs=in_specs,
        out_specs=out_specs,
        cost_estimate=pl.CostEstimate(flops=int(us * 1.1e9), bytes_accessed=1 << 20, transcendentals=0),
        compiler_params=pltpu.CompilerParams(vmem_limit_bytes=grant << 20),
        **kwargs,
    )


def begin(source, target, sem):
    copy = pltpu.make_async_copy(source, target, sem)
    copy.start()
    return copy


def hdot(a, b, contract):
    return lax.dot_general(a, b, (contract, ((), ())), precision=HIGH, preferred_element_type=F32)


def first_half(shape):
    return lax.broadcasted_iota(jnp.int32, shape, len(shape) - 1) < 64


def columns(ref, start, size):
    lead = (slice(None),) * (len(ref.shape) - 1)
    return ref.at[lead + (slice(start, start + size),)]


def quarter_tile(quarter, tile, rows, grad, error):
    odd = lax.rem(quarter, 2)
    first = pl.multiple_of(tile * 512 + (quarter // 2) * 128, 128)
    low, high = pl.ds(first, 128), pl.ds(first + 256, 128)
    low = grad[0, rows, low].astype(F32) + error[0, rows, low].astype(F32)
    high = grad[0, rows, high].astype(F32) + error[0, rows, high].astype(F32)
    return jnp.where(first_half(low.shape), pltpu.roll(low, 64 * odd, 1), pltpu.roll(high, 64 * (1 - odd), 1))


def quarters_kernel(jobs, sizes, grad_in, error_in, *rest):
    count = len(sizes)
    outs, (grad, error), stages = rest[:count], rest[count : count + 2], rest[count + 2 : -2]
    in_sems, out_sems = rest[-2:]
    arrive = []
    for piece in range(4):
        arrive.append(begin(columns(grad_in, piece * 2048, 2048), columns(grad, piece * 2048, 2048), in_sems.at[0, piece]))
        arrive.append(begin(columns(error_in, piece * 2048, 2048), columns(error, piece * 2048, 2048), in_sems.at[1, piece]))
    leave = []
    for piece in range(4):
        arrive[2 * piece].wait()
        arrive[2 * piece + 1].wait()
        for tile in range(4 * piece, 4 * piece + 4):
            cols = slice(tile * 128, tile * 128 + 128)
            for step, start, stop, out, at in jobs:
                quarter = lax.rem(lax.axis_index("x") + step, 4)
                stages[out][at : at + stop - start, cols] = quarter_tile(quarter, tile, slice(start, stop), grad, error)
        for k in range(count):
            source, target = (columns(ref[k], piece * 512, 512) for ref in (stages, outs))
            leave.append(begin(source, target, out_sems.at[k, piece]))
    for copy in leave:
        copy.wait()


def add_kernel(right, left, a, b, upper, lower):
    upper[...] = a[...] + right[...]
    lower[...] = b[...] + left[...]


def partial_kernel(home, upper, lower, out):
    out[:64] = home[:64] + upper[...]
    out[64:] = home[64:] + lower[...]


def left_kernel(home, upper, lower, mine, other, merged, out):
    first = lax.axis_index("core") == 0
    acc = jnp.zeros((256, 256), F32)
    for pair in range(8):
        cols = slice(pair * 256, pair * 256 + 256)
        value = home[:, cols] + jnp.concatenate([upper[:, cols], lower[:, cols]], 0)
        merged[:, cols] = value
        rows = jnp.concatenate(split(value), 0)
        tiles = []
        for tile in (2 * pair, 2 * pair + 1):
            here, there = mine[tile], other[tile]
            tiles += [jnp.where(first, here, there), jnp.where(first, there, here)]
        acc += dot(rows, jnp.concatenate(split(jnp.concatenate(tiles, 0)), 1))
    acc = acc[:128] + acc[128:]
    out[...] = acc[:, :128] + acc[:, 128:]


def stacked(matrix):
    high, low = split(matrix)
    return jnp.concatenate(
        [jnp.concatenate([high, high], 1), jnp.concatenate([low, jnp.zeros_like(low)], 1)], 0
    )


def raw_kernel(p0, p1, p2, p3, merged, own, away, left_out):
    left = total([p0[...], p1[...], p2[...], p3[...]]) * 0.25
    left_out[...] = left
    turned = left.T
    turned = jnp.where(lax.axis_index("core") == 0, turned, jnp.concatenate([turned[64:], turned[:64]], 0))
    rows = stacked(turned)
    gram = lax.dot(turned, left, precision=HIGH, preferred_element_type=F32)
    for step in range(4):
        y = lax.rem(lax.axis_index("y") + step, 4)
        for pair in range(2):
            cols = [pl.ds(pl.multiple_of((4 * z + y) * 128, 128), 128) for z in (2 * pair, 2 * pair + 1)]
            block = jnp.concatenate([merged[:, c] for c in cols], 1)
            block = dot(rows, jnp.concatenate(split(block), 0))
            block = block[:128] + block[128:]
            for k in range(2):
                own[step * 5 + 2 * pair + k] = block[:64, k * 128 : k * 128 + 128]
                away[step * 5 + 2 * pair + k] = block[64:, k * 128 : k * 128 + 128]
        own[step * 5 + 4] = gram[:64]
        away[step * 5 + 4] = gram[64:]


def pack_kernel(own, came, *outs):
    for step in range(4):
        outs[step][...] = own[5 * step : 5 * step + 5] + came[5 * step : 5 * step + 5]


def sum_kernel(p0, p1, p2, p3, out):
    out[...] = total([p0[...], p1[...], p2[...], p3[...]])


def split_kernel(p0, p1, p2, p3, tiles, gram):
    whole = total([p0[...], p1[...], p2[...], p3[...]])
    tiles[...] = whole[:4] * 0.25
    gram[...] = whole[4]


def gather_kernel(p0, p1, p2, p3, out):
    for part, step in ((p0, 0), (p1, 2), (p2, 3), (p3, 1)):
        y = lax.rem(lax.axis_index("y") + step, 4)
        for z in range(4):
            out[z, y] = part[z]


def pair_up(raw, quarters, second):
    lower = first_half((128, 128))
    first, last = (raw[q] for q in quarters)
    if second:
        return jnp.where(lower, pltpu.roll(first, 64, 1), last)
    return jnp.where(lower, first, pltpu.roll(last, 64, 1))


def eliminate(work, starts, size=32):
    below = lax.broadcasted_iota(jnp.int32, (size, 1), 0)
    lane = lax.broadcasted_iota(jnp.int32, (size, 128), 1)
    for start in starts:
        stop = start + size
        panel = work[start:stop, :]
        scales = []
        for j in range(size):
            scale = 1.0 / panel[j : j + 1, start + j : start + j + 1]
            column = jnp.where(below > j, panel[:, start + j : start + j + 1] * scale, 0.0)
            panel = panel - column * panel[j : j + 1, :]
            scales.append(scale)
        scale = jnp.concatenate(scales, 0)
        work[start:stop, :] = panel * lax.sqrt(scale)
        if stop < 128:
            steps = jnp.where(lane >= stop, panel[:, :128] * scale, 0.0)
            work[stop:, :] = work[stop:, :] - hdot(steps, panel, ((0,), (0,)))[stop:]


def begin_factor_kernel(gram, came, work):
    first = lax.axis_index("core") == 0
    gram, came = gram[...], came[...]
    gram = jnp.concatenate([jnp.where(first, gram, came), jnp.where(first, came, gram)], 0)
    row = lax.broadcasted_iota(jnp.int32, (128, 128), 0)
    diagonal = row == lax.broadcasted_iota(jnp.int32, (128, 128), 1)
    eye = jnp.where(diagonal, 1.0, 0.0)
    trace = jnp.sum(jnp.where(diagonal, gram, 0.0))
    work[:, :128] = gram + 1e-06 * trace / 128 * eye
    work[:, 128:] = eye
    eliminate(work, (0,))


def next_factor_kernel(begun, work):
    work[...] = begun[...]
    eliminate(work, (32, 64))


def end_factor_kernel(begun, left, factor, inverse, work):
    work[...] = begun[...]
    eliminate(work, (96,))
    lower = work[:, 128:]
    inverse[...] = lower
    factor[...] = hdot(hdot(left[...], lower, ((1,), (1,))), lower, ((1,), (0,)))


def last_kernel(factor, inverse, *rest):
    raws, (grad, error, momentum, params), outs, right = rest[:8], rest[8:12], rest[12:15], rest[15]
    stages, sems = rest[16:19], rest[19]
    x, z, y = (lax.axis_index(axis) for axis in ("x", "z", "y"))
    first, odd, late = lax.axis_index("core") == 0, lax.rem(x, 2) == 1, x >= 2

    def quarters_of(part, place):
        here, after, before, far = (
            jnp.concatenate([raws[k][part, place], raws[4 + k][part, place]], 0) for k in range(4)
        )
        own = jnp.where(odd, before, here), jnp.where(odd, here, after)
        return own, (jnp.where(odd, after, far), jnp.where(odd, far, before))

    def columns_of(own, other, second):
        own, other = pair_up(own, (0, 1), second), pair_up(other, (0, 1), second)
        return jnp.where(late, other, own), jnp.where(late, own, other)

    weights = factor[...]
    rows = stacked(jnp.where(first, weights, pltpu.roll(weights, 64, 1)))
    leave = []
    for part in range(4):
        for place in range(4):
            own, other = quarters_of(part, place)
            for run in range(2):
                block = jnp.concatenate(columns_of(own, other, run == 1), 1)
                approx = dot(rows, jnp.concatenate(split(block), 0))
                approx = approx[:128] + approx[128:]
                start = part * 2048 + place * 512 + run * 256
                cols = slice(start, start + 256)
                merged = grad[0, :, cols].astype(F32) + error[0, :, cols].astype(F32)
                stages[0][0, :, cols] = (merged - approx).astype(BF16)
                moment = 0.9 * momentum[:, cols].astype(F32) + approx
                stages[1][:, cols] = moment.astype(BF16)
                stages[2][:, cols] = params[:, cols] - 0.7 * (approx + 0.9 * moment)
        for k in range(3):
            source, target = (columns(ref[k], part * 2048, 2048) for ref in (stages, outs))
            leave.append(begin(source, target, sems.at[k, part]))
    own, other = quarters_of(z, y)
    own, other = (
        tuple(jnp.where(first, tile, jnp.concatenate([tile[64:], tile[:64]], 0)) for tile in pair)
        for pair in (own, other)
    )
    halves = zip(columns_of(own, other, False), columns_of(own, other, True))
    for k, (low, high) in enumerate(halves):
        block = hdot(inverse[...], jnp.where(first, low, high), ((1,), (0,)))
        right[k * 128 : k * 128 + 128, :] = block.T
    for copy in leave:
        copy.wait()


def quarters(jobs, sizes, grad, error):
    shapes = [(size, 2048) for size in sizes]
    return call(
        functools.partial(quarters_kernel, jobs, sizes),
        tuple(jax.ShapeDtypeStruct(shape, F32) for shape in shapes),
        [ANY, ANY],
        (ANY,) * len(shapes),
        us=4,
        grant=GRANT,
        scratch_shapes=[pltpu.VMEM((1, 128, 8192), BF16)] * 2
        + [pltpu.VMEM(shape, F32) for shape in shapes]
        + [pltpu.SemaphoreType.DMA((2, 4)), pltpu.SemaphoreType.DMA((len(shapes), 4))],
    )(grad, error)


def local(grad, error, momentum, params, right_factor):
    x = lax.axis_index("x")
    square = jax.ShapeDtypeStruct((128, 128), F32)
    tiles = lambda n: jax.ShapeDtypeStruct((n, 64, 128), F32)

    half, whole = (jax.ShapeDtypeStruct((rows, 2048), F32) for rows in (64, 128))
    a2, b2, b1, a3 = quarters(
        ((2, 0, 64, 0, 0), (2, 64, 128, 1, 0), (1, 64, 128, 2, 0), (3, 0, 64, 3, 0)), (64,) * 4, grad, error
    )
    far_a, far_b = ring(a2, "x", 1), ring(b2, "x", -1)
    b_right, a_left = ring(b1, "x", 1), ring(a3, "x", -1)
    home, a1, b3 = quarters(((0, 0, 128, 0, 0), (1, 0, 64, 1, 0), (3, 64, 128, 2, 0)), (128, 64, 64), grad, error)
    far_a, far_b, home, a1, b3 = lax.optimization_barrier((far_a, far_b, home, a1, b3))
    a1, b3 = call(add_kernel, (half, half), [VMEM] * 4, (VMEM,) * 2, us=0.6)(far_a, far_b, a1, b3)
    a_right, b_left = ring(a1, "x", 1), ring(b3, "x", -1)
    home = call(partial_kernel, whole, [VMEM] * 3, VMEM, us=30)(home, a_left, b_right)

    rows = lax.dynamic_slice_in_dim(right_factor, x * 64, 64, 0)
    mine = lax.all_to_all(jnp.broadcast_to(rows[None], (16, 64, 128)), PLANE, 0, 0)
    other = ring(mine, "core", 1)

    merged, part = call(left_kernel, (whole, square), [VMEM] * 5, (VMEM,) * 2, us=1.2)(
        home, a_right, b_left, mine, other
    )
    parts = exchange(part, "x")
    own, away, left_factor = call(raw_kernel, (tiles(20), tiles(20), square), [VMEM] * 5, (VMEM,) * 3, us=1)(*parts, merged)
    came = ring(away, "core", 1)

    outs = call(pack_kernel, (tiles(5),) * 4, [VMEM] * 2, (VMEM,) * 4, us=0.3)(own, came)
    outs = (outs[0], ring(outs[2], "y", 2), ring(outs[1], "y", 1), ring(outs[3], "y", -1))
    part = call(sum_kernel, tiles(5), [VMEM] * 4, VMEM, us=0.2)(*outs)
    mine, gram = call(split_kernel, (tiles(4), jax.ShapeDtypeStruct((64, 128), F32)), [VMEM] * 4, (VMEM,) * 2, us=0.2)(
        *exchange(part, "z")
    )

    gram_other = ring(gram, "core", 1)
    opposite = ring(mine, "x", 2)
    parts = exchange(mine, "y")
    work = call(begin_factor_kernel, jax.ShapeDtypeStruct((128, 256), F32), [VMEM] * 2, VMEM, us=3.4)(gram, gram_other)
    *parts, opposite, work = lax.optimization_barrier((*parts, opposite, work))
    own = call(gather_kernel, jax.ShapeDtypeStruct((4, 4, 64, 128), F32), [VMEM] * 4, VMEM, us=0.3)(*parts)
    before, after = ring(own, "x", 1), ring(own, "x", -1)
    own_sibling, opposite = lax.optimization_barrier((ring(own, "core", 1), opposite))
    opposite = exchange(opposite, "y")
    own, work = lax.optimization_barrier((own, work))
    block = jax.ShapeDtypeStruct((128, 256), F32)
    work = call(next_factor_kernel, block, [VMEM], VMEM, us=6.2)(work)
    *opposite, work = lax.optimization_barrier((*opposite, work))
    opposite = call(gather_kernel, jax.ShapeDtypeStruct((4, 4, 64, 128), F32), [VMEM] * 4, VMEM, us=0.3)(*opposite)
    before, after, opposite, work = lax.optimization_barrier((before, after, opposite, work))
    raws = (own, after, before, opposite)
    siblings = (own_sibling, *(ring(array, "core", 1) for array in raws[1:]))
    factor, inverse = call(
        end_factor_kernel, (square, square), [VMEM] * 2, (VMEM,) * 2, us=3.4, scratch_shapes=[pltpu.VMEM((128, 256), F32)]
    )(work, left_factor)

    return call(
        last_kernel,
        tuple(jax.ShapeDtypeStruct(array.shape, array.dtype) for array in (error, momentum, params))
        + (jax.ShapeDtypeStruct((256, 128), F32),),
        [VMEM] * 14,
        (ANY,) * 3 + (VMEM,),
        us=7,
        grant=20,
        scratch_shapes=[
            pltpu.VMEM((1, 128, 8192), BF16),
            pltpu.VMEM((128, 8192), BF16),
            pltpu.VMEM((128, 8192), F32),
            pltpu.SemaphoreType.DMA((3, 4)),
        ],
    )(factor, inverse, *raws, *siblings, grad, error, momentum, params)


def solution(mesh):
    fine = Mesh(mesh.devices.reshape(4, 4, 4, 2), ("x", "z", "y", "core"))
    shard = ("z", "y", "core")
    return jax.shard_map(
        local,
        mesh=fine,
        in_specs=(P("x", shard, None), P("x", shard, None), P(shard, None), P(shard, None), P(shard, None)),
        out_specs=(P("x", shard, None), P(shard, None), P(shard, None), P(shard, None)),
        check_vma=False,
    )
```

```python
import functools

import jax
import jax.numpy as jnp
from jax import lax
from jax.experimental import pallas as pl
from jax.experimental.pallas import tpu as pltpu
from jax.sharding import Mesh, PartitionSpec as P

F32 = jnp.float32
BF16 = jnp.bfloat16
HIGH = lax.Precision.HIGHEST
PLANE = ("z", "y")
GRANT = 58
VMEM = pl.BlockSpec(memory_space=pltpu.VMEM)
ANY = pl.BlockSpec(memory_space=pl.ANY)


def split(value):
    high = value.astype(BF16)
    return high, (value - high.astype(F32)).astype(BF16)


def dot(a, b):
    return jnp.dot(a, b, preferred_element_type=F32)


def ring(array, axis, step):
    n = lax.axis_size(axis)
    return lax.ppermute(array, axis, [(i, (i + step) % n) for i in range(n)])


def exchange(array, axis):
    return array, ring(array, axis, 2), ring(array, axis, 1), ring(array, axis, -1)


def total(parts):
    return (parts[0] + parts[1]) + (parts[2] + parts[3])


def call(kernel, out_shape, in_specs, out_specs, us, grant=12, **kwargs):
    return pl.pallas_call(
        kernel,
        out_shape=out_shape,
        in_specs=in_specs,
        out_specs=out_specs,
        cost_estimate=pl.CostEstimate(flops=int(us * 1.1e9), bytes_accessed=1 << 20, transcendentals=0),
        compiler_params=pltpu.CompilerParams(vmem_limit_bytes=grant << 20),
        **kwargs,
    )


def begin(source, target, sem):
    copy = pltpu.make_async_copy(source, target, sem)
    copy.start()
    return copy


def hdot(a, b, contract):
    return lax.dot_general(a, b, (contract, ((), ())), precision=HIGH, preferred_element_type=F32)


def first_half(shape):
    return lax.broadcasted_iota(jnp.int32, shape, len(shape) - 1) < 64


def columns(ref, start, size):
    lead = (slice(None),) * (len(ref.shape) - 1)
    return ref.at[lead + (slice(start, start + size),)]


def quarter_tile(quarter, tile, rows, grad, error):
    odd = lax.rem(quarter, 2)
    first = pl.multiple_of(tile * 512 + (quarter // 2) * 128, 128)
    low, high = pl.ds(first, 128), pl.ds(first + 256, 128)
    low = grad[0, rows, low].astype(F32) + error[0, rows, low].astype(F32)
    high = grad[0, rows, high].astype(F32) + error[0, rows, high].astype(F32)
    return jnp.where(first_half(low.shape), pltpu.roll(low, 64 * odd, 1), pltpu.roll(high, 64 * (1 - odd), 1))


def quarters_kernel(jobs, sizes, grad_in, error_in, *rest):
    count = len(sizes)
    outs, (grad, error), stages = rest[:count], rest[count : count + 2], rest[count + 2 : -2]
    in_sems, out_sems = rest[-2:]
    arrive = []
    for piece in range(4):
        arrive.append(begin(columns(grad_in, piece * 2048, 2048), columns(grad, piece * 2048, 2048), in_sems.at[0, piece]))
        arrive.append(begin(columns(error_in, piece * 2048, 2048), columns(error, piece * 2048, 2048), in_sems.at[1, piece]))
    leave = []
    for piece in range(4):
        arrive[2 * piece].wait()
        arrive[2 * piece + 1].wait()
        for tile in range(4 * piece, 4 * piece + 4):
            cols = slice(tile * 128, tile * 128 + 128)
            for step, start, stop, out, at in jobs:
                quarter = lax.rem(lax.axis_index("x") + step, 4)
                stages[out][at : at + stop - start, cols] = quarter_tile(quarter, tile, slice(start, stop), grad, error)
        for k in range(count):
            source, target = (columns(ref[k], piece * 512, 512) for ref in (stages, outs))
            leave.append(begin(source, target, out_sems.at[k, piece]))
    for copy in leave:
        copy.wait()


def add_kernel(right, left, a, b, upper, lower):
    upper[...] = a[...] + right[...]
    lower[...] = b[...] + left[...]


def partial_kernel(home, upper, lower, out):
    out[:64] = home[:64] + upper[...]
    out[64:] = home[64:] + lower[...]


def left_kernel(home, upper, lower, mine, other, merged, out):
    first = lax.axis_index("core") == 0
    acc = jnp.zeros((256, 256), F32)
    for pair in range(8):
        cols = slice(pair * 256, pair * 256 + 256)
        value = home[:, cols] + jnp.concatenate([upper[:, cols], lower[:, cols]], 0)
        merged[:, cols] = value
        rows = jnp.concatenate(split(value), 0)
        tiles = []
        for tile in (2 * pair, 2 * pair + 1):
            here, there = mine[tile], other[tile]
            tiles += [jnp.where(first, here, there), jnp.where(first, there, here)]
        acc += dot(rows, jnp.concatenate(split(jnp.concatenate(tiles, 0)), 1))
    acc = acc[:128] + acc[128:]
    out[...] = acc[:, :128] + acc[:, 128:]


def stacked(matrix):
    high, low = split(matrix)
    return jnp.concatenate(
        [jnp.concatenate([high, high], 1), jnp.concatenate([low, jnp.zeros_like(low)], 1)], 0
    )


def raw_kernel(p0, p1, p2, p3, merged, own, away, left_out):
    left = total([p0[...], p1[...], p2[...], p3[...]]) * 0.25
    left_out[...] = left
    turned = left.T
    turned = jnp.where(lax.axis_index("core") == 0, turned, jnp.concatenate([turned[64:], turned[:64]], 0))
    rows = stacked(turned)
    gram = lax.dot(turned, left, precision=HIGH, preferred_element_type=F32)
    for step in range(4):
        y = lax.rem(lax.axis_index("y") + step, 4)
        for pair in range(2):
            cols = [pl.ds(pl.multiple_of((4 * z + y) * 128, 128), 128) for z in (2 * pair, 2 * pair + 1)]
            block = jnp.concatenate([merged[:, c] for c in cols], 1)
            block = dot(rows, jnp.concatenate(split(block), 0))
            block = block[:128] + block[128:]
            for k in range(2):
                own[step * 5 + 2 * pair + k] = block[:64, k * 128 : k * 128 + 128]
                away[step * 5 + 2 * pair + k] = block[64:, k * 128 : k * 128 + 128]
        own[step * 5 + 4] = gram[:64]
        away[step * 5 + 4] = gram[64:]


def pack_kernel(own, came, *outs):
    for step in range(4):
        outs[step][...] = own[5 * step : 5 * step + 5] + came[5 * step : 5 * step + 5]


def sum_kernel(p0, p1, p2, p3, out):
    out[...] = total([p0[...], p1[...], p2[...], p3[...]])


def split_kernel(p0, p1, p2, p3, tiles, gram):
    whole = total([p0[...], p1[...], p2[...], p3[...]])
    tiles[...] = whole[:4] * 0.25
    gram[...] = whole[4]


def gather_kernel(p0, p1, p2, p3, out):
    for part, step in ((p0, 0), (p1, 2), (p2, 3), (p3, 1)):
        y = lax.rem(lax.axis_index("y") + step, 4)
        for z in range(4):
            out[z, y] = part[z]


def pair_up(raw, quarters, second):
    lower = first_half((128, 128))
    first, last = (raw[q] for q in quarters)
    if second:
        return jnp.where(lower, pltpu.roll(first, 64, 1), last)
    return jnp.where(lower, first, pltpu.roll(last, 64, 1))


def eliminate(work, starts, size=32):
    below = lax.broadcasted_iota(jnp.int32, (size, 1), 0)
    lane = lax.broadcasted_iota(jnp.int32, (size, 128), 1)
    for start in starts:
        stop = start + size
        panel = work[start:stop, :]
        scales = []
        for j in range(size):
            scale = 1.0 / panel[j : j + 1, start + j : start + j + 1]
            column = jnp.where(below > j, panel[:, start + j : start + j + 1] * scale, 0.0)
            panel = panel - column * panel[j : j + 1, :]
            scales.append(scale)
        scale = jnp.concatenate(scales, 0)
        work[start:stop, :] = panel * lax.sqrt(scale)
        if stop < 128:
            steps = jnp.where(lane >= stop, panel[:, :128] * scale, 0.0)
            work[stop:, :] = work[stop:, :] - hdot(steps, panel, ((0,), (0,)))[stop:]


def begin_factor_kernel(gram, came, work):
    first = lax.axis_index("core") == 0
    gram, came = gram[...], came[...]
    gram = jnp.concatenate([jnp.where(first, gram, came), jnp.where(first, came, gram)], 0)
    row = lax.broadcasted_iota(jnp.int32, (128, 128), 0)
    diagonal = row == lax.broadcasted_iota(jnp.int32, (128, 128), 1)
    eye = jnp.where(diagonal, 1.0, 0.0)
    trace = jnp.sum(jnp.where(diagonal, gram, 0.0))
    work[:, :128] = gram + 1e-06 * trace / 128 * eye
    work[:, 128:] = eye
    eliminate(work, (0,))


def next_factor_kernel(begun, work):
    work[...] = begun[...]
    eliminate(work, (32, 64))


def end_factor_kernel(begun, left, factor, inverse, work):
    work[...] = begun[...]
    eliminate(work, (96,))
    lower = work[:, 128:]
    inverse[...] = lower
    factor[...] = hdot(hdot(left[...], lower, ((1,), (1,))), lower, ((1,), (0,)))


def last_kernel(factor, inverse, *rest):
    raws, (grad, error, momentum, params), outs, right = rest[:8], rest[8:12], rest[12:15], rest[15]
    stages, sems = rest[16:19], rest[19]
    x, z, y = (lax.axis_index(axis) for axis in ("x", "z", "y"))
    first, odd, late = lax.axis_index("core") == 0, lax.rem(x, 2) == 1, x >= 2

    def quarters_of(part, place):
        here, after, before, far = (
            jnp.concatenate([raws[k][part, place], raws[4 + k][part, place]], 0) for k in range(4)
        )
        own = jnp.where(odd, before, here), jnp.where(odd, here, after)
        return own, (jnp.where(odd, after, far), jnp.where(odd, far, before))

    def columns_of(own, other, second):
        own, other = pair_up(own, (0, 1), second), pair_up(other, (0, 1), second)
        return jnp.where(late, other, own), jnp.where(late, own, other)

    weights = factor[...]
    rows = stacked(jnp.where(first, weights, pltpu.roll(weights, 64, 1)))
    leave = []
    for part in range(4):
        for place in range(4):
            own, other = quarters_of(part, place)
            for run in range(2):
                block = jnp.concatenate(columns_of(own, other, run == 1), 1)
                approx = dot(rows, jnp.concatenate(split(block), 0))
                approx = approx[:128] + approx[128:]
                start = part * 2048 + place * 512 + run * 256
                cols = slice(start, start + 256)
                merged = grad[0, :, cols].astype(F32) + error[0, :, cols].astype(F32)
                stages[0][0, :, cols] = (merged - approx).astype(BF16)
                moment = 0.9 * momentum[:, cols].astype(F32) + approx
                stages[1][:, cols] = moment.astype(BF16)
                stages[2][:, cols] = params[:, cols] - 0.7 * (approx + 0.9 * moment)
            if place % 2 == 1:
                for k in range(3):
                    start = part * 2048 + (place - 1) * 512
                    source, target = (columns(ref[k], start, 1024) for ref in (stages, outs))
                    leave.append(begin(source, target, sems.at[k, 2 * part + place // 2]))
    own, other = quarters_of(z, y)
    own, other = (
        tuple(jnp.where(first, tile, jnp.concatenate([tile[64:], tile[:64]], 0)) for tile in pair)
        for pair in (own, other)
    )
    halves = zip(columns_of(own, other, False), columns_of(own, other, True))
    for k, (low, high) in enumerate(halves):
        block = hdot(inverse[...], jnp.where(first, low, high), ((1,), (0,)))
        right[k * 128 : k * 128 + 128, :] = block.T
    for copy in leave:
        copy.wait()


def quarters(jobs, sizes, grad, error):
    shapes = [(size, 2048) for size in sizes]
    return call(
        functools.partial(quarters_kernel, jobs, sizes),
        tuple(jax.ShapeDtypeStruct(shape, F32) for shape in shapes),
        [ANY, ANY],
        (ANY,) * len(shapes),
        us=4,
        grant=GRANT,
        scratch_shapes=[pltpu.VMEM((1, 128, 8192), BF16)] * 2
        + [pltpu.VMEM(shape, F32) for shape in shapes]
        + [pltpu.SemaphoreType.DMA((2, 4)), pltpu.SemaphoreType.DMA((len(shapes), 4))],
    )(grad, error)


def local(grad, error, momentum, params, right_factor):
    x = lax.axis_index("x")
    square = jax.ShapeDtypeStruct((128, 128), F32)
    tiles = lambda n: jax.ShapeDtypeStruct((n, 64, 128), F32)

    half, whole = (jax.ShapeDtypeStruct((rows, 2048), F32) for rows in (64, 128))
    a2, b2, b1, a3 = quarters(
        ((2, 0, 64, 0, 0), (2, 64, 128, 1, 0), (1, 64, 128, 2, 0), (3, 0, 64, 3, 0)), (64,) * 4, grad, error
    )
    far_a, far_b = ring(a2, "x", 1), ring(b2, "x", -1)
    b_right, a_left = ring(b1, "x", 1), ring(a3, "x", -1)
    home, a1, b3 = quarters(((0, 0, 128, 0, 0), (1, 0, 64, 1, 0), (3, 64, 128, 2, 0)), (128, 64, 64), grad, error)
    far_a, far_b, home, a1, b3 = lax.optimization_barrier((far_a, far_b, home, a1, b3))
    a1, b3 = call(add_kernel, (half, half), [VMEM] * 4, (VMEM,) * 2, us=0.6)(far_a, far_b, a1, b3)
    a_right, b_left = ring(a1, "x", 1), ring(b3, "x", -1)
    home = call(partial_kernel, whole, [VMEM] * 3, VMEM, us=30)(home, a_left, b_right)

    rows = lax.dynamic_slice_in_dim(right_factor, x * 64, 64, 0)
    mine = lax.all_to_all(jnp.broadcast_to(rows[None], (16, 64, 128)), PLANE, 0, 0)
    other = ring(mine, "core", 1)

    merged, part = call(left_kernel, (whole, square), [VMEM] * 5, (VMEM,) * 2, us=1.2)(
        home, a_right, b_left, mine, other
    )
    parts = exchange(part, "x")
    own, away, left_factor = call(raw_kernel, (tiles(20), tiles(20), square), [VMEM] * 5, (VMEM,) * 3, us=1)(*parts, merged)
    came = ring(away, "core", 1)

    outs = call(pack_kernel, (tiles(5),) * 4, [VMEM] * 2, (VMEM,) * 4, us=0.3)(own, came)
    outs = (outs[0], ring(outs[2], "y", 2), ring(outs[1], "y", 1), ring(outs[3], "y", -1))
    part = call(sum_kernel, tiles(5), [VMEM] * 4, VMEM, us=0.2)(*outs)
    mine, gram = call(split_kernel, (tiles(4), jax.ShapeDtypeStruct((64, 128), F32)), [VMEM] * 4, (VMEM,) * 2, us=0.2)(
        *exchange(part, "z")
    )

    gram_other = ring(gram, "core", 1)
    parts = exchange(mine, "y")
    mine, gram_other = lax.optimization_barrier((mine, gram_other))
    opposite = ring(mine, "x", 2)
    work = call(begin_factor_kernel, jax.ShapeDtypeStruct((128, 256), F32), [VMEM] * 2, VMEM, us=3.4)(gram, gram_other)
    *parts, opposite, work = lax.optimization_barrier((*parts, opposite, work))
    own = call(gather_kernel, jax.ShapeDtypeStruct((4, 4, 64, 128), F32), [VMEM] * 4, VMEM, us=0.3)(*parts)
    before, after = ring(own, "x", 1), ring(own, "x", -1)
    own_sibling, opposite = lax.optimization_barrier((ring(own, "core", 1), opposite))
    opposite = exchange(opposite, "y")
    own, work = lax.optimization_barrier((own, work))
    block = jax.ShapeDtypeStruct((128, 256), F32)
    work = call(next_factor_kernel, block, [VMEM], VMEM, us=6.2)(work)
    *opposite, work = lax.optimization_barrier((*opposite, work))
    opposite = call(gather_kernel, jax.ShapeDtypeStruct((4, 4, 64, 128), F32), [VMEM] * 4, VMEM, us=0.3)(*opposite)
    opposite_sibling = ring(opposite, "core", 1)
    factor, inverse = call(
        end_factor_kernel, (square, square), [VMEM] * 2, (VMEM,) * 2, us=3.4, scratch_shapes=[pltpu.VMEM((128, 256), F32)]
    )(work, left_factor)
    before, after, opposite_sibling, factor, inverse = lax.optimization_barrier(
        (before, after, opposite_sibling, factor, inverse)
    )
    raws = (own, after, before, opposite)
    siblings = (own_sibling, ring(after, "core", 1), ring(before, "core", 1), opposite_sibling)

    return call(
        last_kernel,
        tuple(jax.ShapeDtypeStruct(array.shape, array.dtype) for array in (error, momentum, params))
        + (jax.ShapeDtypeStruct((256, 128), F32),),
        [VMEM] * 14,
        (ANY,) * 3 + (VMEM,),
        us=7,
        grant=20,
        scratch_shapes=[
            pltpu.VMEM((1, 128, 8192), BF16),
            pltpu.VMEM((128, 8192), BF16),
            pltpu.VMEM((128, 8192), F32),
            pltpu.SemaphoreType.DMA((3, 8)),
        ],
    )(factor, inverse, *raws, *siblings, grad, error, momentum, params)


def solution(mesh):
    fine = Mesh(mesh.devices.reshape(4, 4, 4, 2), ("x", "z", "y", "core"))
    shard = ("z", "y", "core")
    return jax.shard_map(
        local,
        mesh=fine,
        in_specs=(P("x", shard, None), P("x", shard, None), P(shard, None), P(shard, None), P(shard, None)),
        out_specs=(P("x", shard, None), P(shard, None), P(shard, None), P(shard, None)),
        check_vma=False,
    )
```

```python
import functools

import jax
import jax.numpy as jnp
from jax import lax
from jax.experimental import pallas as pl
from jax.experimental.pallas import tpu as pltpu
from jax.sharding import Mesh, PartitionSpec as P

F32 = jnp.float32
BF16 = jnp.bfloat16
HIGH = lax.Precision.HIGHEST
PLANE = ("z", "y")
GRANT = 58
VMEM = pl.BlockSpec(memory_space=pltpu.VMEM)
ANY = pl.BlockSpec(memory_space=pl.ANY)


def split(value):
    high = value.astype(BF16)
    return high, (value - high.astype(F32)).astype(BF16)


def dot(a, b):
    return jnp.dot(a, b, preferred_element_type=F32)


def ring(array, axis, step):
    n = lax.axis_size(axis)
    return lax.ppermute(array, axis, [(i, (i + step) % n) for i in range(n)])


def exchange(array, axis):
    return array, ring(array, axis, 2), ring(array, axis, 1), ring(array, axis, -1)


def total(parts):
    return (parts[0] + parts[1]) + (parts[2] + parts[3])


def call(kernel, out_shape, in_specs, out_specs, us, grant=12, **kwargs):
    return pl.pallas_call(
        kernel,
        out_shape=out_shape,
        in_specs=in_specs,
        out_specs=out_specs,
        cost_estimate=pl.CostEstimate(flops=int(us * 1.1e9), bytes_accessed=1 << 20, transcendentals=0),
        compiler_params=pltpu.CompilerParams(vmem_limit_bytes=grant << 20),
        **kwargs,
    )


def begin(source, target, sem):
    copy = pltpu.make_async_copy(source, target, sem)
    copy.start()
    return copy


def hdot(a, b, contract):
    return lax.dot_general(a, b, (contract, ((), ())), precision=HIGH, preferred_element_type=F32)


def first_half(shape):
    return lax.broadcasted_iota(jnp.int32, shape, len(shape) - 1) < 64


def columns(ref, start, size):
    lead = (slice(None),) * (len(ref.shape) - 1)
    return ref.at[lead + (slice(start, start + size),)]


def quarter_tile(quarter, tile, rows, grad, error):
    odd = lax.rem(quarter, 2)
    first = pl.multiple_of(tile * 512 + (quarter // 2) * 128, 128)
    low, high = pl.ds(first, 128), pl.ds(first + 256, 128)
    low = grad[0, rows, low].astype(F32) + error[0, rows, low].astype(F32)
    high = grad[0, rows, high].astype(F32) + error[0, rows, high].astype(F32)
    return jnp.where(first_half(low.shape), pltpu.roll(low, 64 * odd, 1), pltpu.roll(high, 64 * (1 - odd), 1))


def quarters_kernel(jobs, sizes, grad_in, error_in, *rest):
    count = len(sizes)
    outs, (grad, error), stages = rest[:count], rest[count : count + 2], rest[count + 2 : -2]
    in_sems, out_sems = rest[-2:]
    arrive = []
    for piece in range(2):
        arrive.append(begin(columns(grad_in, piece * 4096, 4096), columns(grad, piece * 4096, 4096), in_sems.at[0, piece]))
        arrive.append(begin(columns(error_in, piece * 4096, 4096), columns(error, piece * 4096, 4096), in_sems.at[1, piece]))
    leave = []
    for piece in range(2):
        arrive[2 * piece].wait()
        arrive[2 * piece + 1].wait()
        for tile in range(8 * piece, 8 * piece + 8):
            cols = slice(tile * 128, tile * 128 + 128)
            for step, start, stop, out, at in jobs:
                quarter = lax.rem(lax.axis_index("x") + step, 4)
                stages[out][at : at + stop - start, cols] = quarter_tile(quarter, tile, slice(start, stop), grad, error)
        for k in range(count):
            source, target = (columns(ref[k], piece * 1024, 1024) for ref in (stages, outs))
            leave.append(begin(source, target, out_sems.at[k, piece]))
    for copy in leave:
        copy.wait()


def add_kernel(right, left, a, b, upper, lower):
    upper[...] = a[...] + right[...]
    lower[...] = b[...] + left[...]


def partial_kernel(home, upper, lower, out):
    out[:64] = home[:64] + upper[...]
    out[64:] = home[64:] + lower[...]


def left_kernel(home, upper, lower, mine, other, merged, out):
    first = lax.axis_index("core") == 0
    acc = jnp.zeros((256, 256), F32)
    for pair in range(8):
        cols = slice(pair * 256, pair * 256 + 256)
        value = home[:, cols] + jnp.concatenate([upper[:, cols], lower[:, cols]], 0)
        merged[:, cols] = value
        rows = jnp.concatenate(split(value), 0)
        tiles = []
        for tile in (2 * pair, 2 * pair + 1):
            here, there = mine[tile], other[tile]
            tiles += [jnp.where(first, here, there), jnp.where(first, there, here)]
        acc += dot(rows, jnp.concatenate(split(jnp.concatenate(tiles, 0)), 1))
    acc = acc[:128] + acc[128:]
    out[...] = acc[:, :128] + acc[:, 128:]


def stacked(matrix):
    high, low = split(matrix)
    return jnp.concatenate(
        [jnp.concatenate([high, high], 1), jnp.concatenate([low, jnp.zeros_like(low)], 1)], 0
    )


def raw_kernel(p0, p1, p2, p3, merged, own, away, left_out):
    left = total([p0[...], p1[...], p2[...], p3[...]]) * 0.25
    left_out[...] = left
    turned = left.T
    turned = jnp.where(lax.axis_index("core") == 0, turned, jnp.concatenate([turned[64:], turned[:64]], 0))
    rows = stacked(turned)
    gram = lax.dot(turned, left, precision=HIGH, preferred_element_type=F32)
    for step in range(4):
        y = lax.rem(lax.axis_index("y") + step, 4)
        for pair in range(2):
            cols = [pl.ds(pl.multiple_of((4 * z + y) * 128, 128), 128) for z in (2 * pair, 2 * pair + 1)]
            block = jnp.concatenate([merged[:, c] for c in cols], 1)
            block = dot(rows, jnp.concatenate(split(block), 0))
            block = block[:128] + block[128:]
            for k in range(2):
                own[step * 5 + 2 * pair + k] = block[:64, k * 128 : k * 128 + 128]
                away[step * 5 + 2 * pair + k] = block[64:, k * 128 : k * 128 + 128]
        own[step * 5 + 4] = gram[:64]
        away[step * 5 + 4] = gram[64:]


def pack_kernel(own, came, *outs):
    for step in range(4):
        outs[step][...] = own[5 * step : 5 * step + 5] + came[5 * step : 5 * step + 5]


def sum_kernel(p0, p1, p2, p3, out):
    out[...] = total([p0[...], p1[...], p2[...], p3[...]])


def split_kernel(p0, p1, p2, p3, tiles, gram):
    whole = total([p0[...], p1[...], p2[...], p3[...]])
    tiles[...] = whole[:4] * 0.25
    gram[...] = whole[4]


def gather_kernel(p0, p1, p2, p3, out):
    for part, step in ((p0, 0), (p1, 2), (p2, 3), (p3, 1)):
        y = lax.rem(lax.axis_index("y") + step, 4)
        for z in range(4):
            out[z, y] = part[z]


def pair_up(raw, quarters, second):
    lower = first_half((128, 128))
    first, last = (raw[q] for q in quarters)
    if second:
        return jnp.where(lower, pltpu.roll(first, 64, 1), last)
    return jnp.where(lower, first, pltpu.roll(last, 64, 1))


def eliminate(work, starts, size=32):
    below = lax.broadcasted_iota(jnp.int32, (size, 1), 0)
    lane = lax.broadcasted_iota(jnp.int32, (size, 128), 1)
    for start in starts:
        stop = start + size
        panel = work[start:stop, :]
        scales = []
        for j in range(size):
            scale = 1.0 / panel[j : j + 1, start + j : start + j + 1]
            column = jnp.where(below > j, panel[:, start + j : start + j + 1] * scale, 0.0)
            panel = panel - column * panel[j : j + 1, :]
            scales.append(scale)
        scale = jnp.concatenate(scales, 0)
        work[start:stop, :] = panel * lax.sqrt(scale)
        if stop < 128:
            steps = jnp.where(lane >= stop, panel[:, :128] * scale, 0.0)
            work[stop:, :] = work[stop:, :] - hdot(steps, panel, ((0,), (0,)))[stop:]


def begin_factor_kernel(gram, came, work):
    first = lax.axis_index("core") == 0
    gram, came = gram[...], came[...]
    gram = jnp.concatenate([jnp.where(first, gram, came), jnp.where(first, came, gram)], 0)
    row = lax.broadcasted_iota(jnp.int32, (128, 128), 0)
    diagonal = row == lax.broadcasted_iota(jnp.int32, (128, 128), 1)
    eye = jnp.where(diagonal, 1.0, 0.0)
    trace = jnp.sum(jnp.where(diagonal, gram, 0.0))
    work[:, :128] = gram + 1e-06 * trace / 128 * eye
    work[:, 128:] = eye
    eliminate(work, (0,))


def next_factor_kernel(begun, work):
    work[...] = begun[...]
    eliminate(work, (32, 64))


def end_factor_kernel(begun, left, factor, inverse, work):
    work[...] = begun[...]
    eliminate(work, (96,))
    lower = work[:, 128:]
    inverse[...] = lower
    factor[...] = hdot(hdot(left[...], lower, ((1,), (1,))), lower, ((1,), (0,)))


def last_kernel(factor, inverse, *rest):
    raws, (grad, error, momentum, params), outs, right = rest[:8], rest[8:12], rest[12:15], rest[15]
    stages, sems = rest[16:19], rest[19]
    x, z, y = (lax.axis_index(axis) for axis in ("x", "z", "y"))
    first, odd, late = lax.axis_index("core") == 0, lax.rem(x, 2) == 1, x >= 2

    def quarters_of(part, place):
        here, after, before, far = (
            jnp.concatenate([raws[k][part, place], raws[4 + k][part, place]], 0) for k in range(4)
        )
        own = jnp.where(odd, before, here), jnp.where(odd, here, after)
        return own, (jnp.where(odd, after, far), jnp.where(odd, far, before))

    def columns_of(own, other, second):
        own, other = pair_up(own, (0, 1), second), pair_up(other, (0, 1), second)
        return jnp.where(late, other, own), jnp.where(late, own, other)

    weights = factor[...]
    rows = stacked(jnp.where(first, weights, pltpu.roll(weights, 64, 1)))
    leave = []
    for part in range(4):
        for place in range(4):
            own, other = quarters_of(part, place)
            for run in range(2):
                block = jnp.concatenate(columns_of(own, other, run == 1), 1)
                approx = dot(rows, jnp.concatenate(split(block), 0))
                approx = approx[:128] + approx[128:]
                start = part * 2048 + place * 512 + run * 256
                cols = slice(start, start + 256)
                merged = grad[0, :, cols].astype(F32) + error[0, :, cols].astype(F32)
                stages[0][0, :, cols] = (merged - approx).astype(BF16)
                moment = 0.9 * momentum[:, cols].astype(F32) + approx
                stages[1][:, cols] = moment.astype(BF16)
                stages[2][:, cols] = params[:, cols] - 0.7 * (approx + 0.9 * moment)
            if place % 2 == 1:
                for k in range(3):
                    start = part * 2048 + (place - 1) * 512
                    source, target = (columns(ref[k], start, 1024) for ref in (stages, outs))
                    leave.append(begin(source, target, sems.at[k, 2 * part + place // 2]))
    own, other = quarters_of(z, y)
    own, other = (
        tuple(jnp.where(first, tile, jnp.concatenate([tile[64:], tile[:64]], 0)) for tile in pair)
        for pair in (own, other)
    )
    halves = zip(columns_of(own, other, False), columns_of(own, other, True))
    for k, (low, high) in enumerate(halves):
        block = hdot(inverse[...], jnp.where(first, low, high), ((1,), (0,)))
        right[k * 128 : k * 128 + 128, :] = block.T
    for copy in leave:
        copy.wait()


def quarters(jobs, sizes, grad, error):
    shapes = [(size, 2048) for size in sizes]
    return call(
        functools.partial(quarters_kernel, jobs, sizes),
        tuple(jax.ShapeDtypeStruct(shape, F32) for shape in shapes),
        [ANY, ANY],
        (ANY,) * len(shapes),
        us=4,
        grant=GRANT,
        scratch_shapes=[pltpu.VMEM((1, 128, 8192), BF16)] * 2
        + [pltpu.VMEM(shape, F32) for shape in shapes]
        + [pltpu.SemaphoreType.DMA((2, 2)), pltpu.SemaphoreType.DMA((len(shapes), 2))],
    )(grad, error)


def local(grad, error, momentum, params, right_factor):
    x = lax.axis_index("x")
    square = jax.ShapeDtypeStruct((128, 128), F32)
    tiles = lambda n: jax.ShapeDtypeStruct((n, 64, 128), F32)

    half, whole = (jax.ShapeDtypeStruct((rows, 2048), F32) for rows in (64, 128))
    a2, b2, b1, a3 = quarters(
        ((2, 0, 64, 0, 0), (2, 64, 128, 1, 0), (1, 64, 128, 2, 0), (3, 0, 64, 3, 0)), (64,) * 4, grad, error
    )
    far_a, far_b = ring(a2, "x", 1), ring(b2, "x", -1)
    b_right, a_left = ring(b1, "x", 1), ring(a3, "x", -1)
    home, a1, b3 = quarters(((0, 0, 128, 0, 0), (1, 0, 64, 1, 0), (3, 64, 128, 2, 0)), (128, 64, 64), grad, error)
    far_a, far_b, home, a1, b3 = lax.optimization_barrier((far_a, far_b, home, a1, b3))
    a1, b3 = call(add_kernel, (half, half), [VMEM] * 4, (VMEM,) * 2, us=0.6)(far_a, far_b, a1, b3)
    a_right, b_left = ring(a1, "x", 1), ring(b3, "x", -1)
    home = call(partial_kernel, whole, [VMEM] * 3, VMEM, us=30)(home, a_left, b_right)

    rows = lax.dynamic_slice_in_dim(right_factor, x * 64, 64, 0)
    mine = lax.all_to_all(jnp.broadcast_to(rows[None], (16, 64, 128)), PLANE, 0, 0)
    other = ring(mine, "core", 1)

    merged, part = call(left_kernel, (whole, square), [VMEM] * 5, (VMEM,) * 2, us=1.2)(
        home, a_right, b_left, mine, other
    )
    parts = exchange(part, "x")
    own, away, left_factor = call(raw_kernel, (tiles(20), tiles(20), square), [VMEM] * 5, (VMEM,) * 3, us=1)(*parts, merged)
    came = ring(away, "core", 1)

    outs = call(pack_kernel, (tiles(5),) * 4, [VMEM] * 2, (VMEM,) * 4, us=0.3)(own, came)
    outs = (outs[0], ring(outs[2], "y", 2), ring(outs[1], "y", 1), ring(outs[3], "y", -1))
    part = call(sum_kernel, tiles(5), [VMEM] * 4, VMEM, us=0.2)(*outs)
    mine, gram = call(split_kernel, (tiles(4), jax.ShapeDtypeStruct((64, 128), F32)), [VMEM] * 4, (VMEM,) * 2, us=0.2)(
        *exchange(part, "z")
    )

    gram_other = ring(gram, "core", 1)
    parts = exchange(mine, "y")
    mine, gram_other = lax.optimization_barrier((mine, gram_other))
    opposite = ring(mine, "x", 2)
    work = call(begin_factor_kernel, jax.ShapeDtypeStruct((128, 256), F32), [VMEM] * 2, VMEM, us=3.4)(gram, gram_other)
    *parts, opposite, work = lax.optimization_barrier((*parts, opposite, work))
    own = call(gather_kernel, jax.ShapeDtypeStruct((4, 4, 64, 128), F32), [VMEM] * 4, VMEM, us=0.3)(*parts)
    before, after = ring(own, "x", 1), ring(own, "x", -1)
    own_sibling, opposite = lax.optimization_barrier((ring(own, "core", 1), opposite))
    opposite = exchange(opposite, "y")
    own, work = lax.optimization_barrier((own, work))
    block = jax.ShapeDtypeStruct((128, 256), F32)
    work = call(next_factor_kernel, block, [VMEM], VMEM, us=6.2)(work)
    *opposite, work = lax.optimization_barrier((*opposite, work))
    opposite = call(gather_kernel, jax.ShapeDtypeStruct((4, 4, 64, 128), F32), [VMEM] * 4, VMEM, us=0.3)(*opposite)
    opposite_sibling = ring(opposite, "core", 1)
    factor, inverse = call(
        end_factor_kernel, (square, square), [VMEM] * 2, (VMEM,) * 2, us=3.4, scratch_shapes=[pltpu.VMEM((128, 256), F32)]
    )(work, left_factor)
    before, after, opposite_sibling, factor, inverse = lax.optimization_barrier(
        (before, after, opposite_sibling, factor, inverse)
    )
    raws = (own, after, before, opposite)
    siblings = (own_sibling, ring(after, "core", 1), ring(before, "core", 1), opposite_sibling)

    return call(
        last_kernel,
        tuple(jax.ShapeDtypeStruct(array.shape, array.dtype) for array in (error, momentum, params))
        + (jax.ShapeDtypeStruct((256, 128), F32),),
        [VMEM] * 14,
        (ANY,) * 3 + (VMEM,),
        us=7,
        grant=20,
        scratch_shapes=[
            pltpu.VMEM((1, 128, 8192), BF16),
            pltpu.VMEM((128, 8192), BF16),
            pltpu.VMEM((128, 8192), F32),
            pltpu.SemaphoreType.DMA((3, 8)),
        ],
    )(factor, inverse, *raws, *siblings, grad, error, momentum, params)


def solution(mesh):
    fine = Mesh(mesh.devices.reshape(4, 4, 4, 2), ("x", "z", "y", "core"))
    shard = ("z", "y", "core")
    return jax.shard_map(
        local,
        mesh=fine,
        in_specs=(P("x", shard, None), P("x", shard, None), P(shard, None), P(shard, None), P(shard, None)),
        out_specs=(P("x", shard, None), P(shard, None), P(shard, None), P(shard, None)),
        check_vma=False,
    )
```

```python
import functools

import jax
import jax.numpy as jnp
from jax import lax
from jax.experimental import pallas as pl
from jax.experimental.pallas import tpu as pltpu
from jax.sharding import Mesh, PartitionSpec as P

F32 = jnp.float32
BF16 = jnp.bfloat16
HIGH = lax.Precision.HIGHEST
PLANE = ("z", "y")
GRANT = 58
VMEM = pl.BlockSpec(memory_space=pltpu.VMEM)
ANY = pl.BlockSpec(memory_space=pl.ANY)


def split(value):
    high = value.astype(BF16)
    return high, (value - high.astype(F32)).astype(BF16)


def dot(a, b):
    return jnp.dot(a, b, preferred_element_type=F32)


def ring(array, axis, step):
    n = lax.axis_size(axis)
    return lax.ppermute(array, axis, [(i, (i + step) % n) for i in range(n)])


def exchange(array, axis):
    return array, ring(array, axis, 2), ring(array, axis, 1), ring(array, axis, -1)


def total(parts):
    return (parts[0] + parts[1]) + (parts[2] + parts[3])


def call(kernel, out_shape, in_specs, out_specs, us, grant=12, **kwargs):
    return pl.pallas_call(
        kernel,
        out_shape=out_shape,
        in_specs=in_specs,
        out_specs=out_specs,
        cost_estimate=pl.CostEstimate(flops=int(us * 1.1e9), bytes_accessed=1 << 20, transcendentals=0),
        compiler_params=pltpu.CompilerParams(vmem_limit_bytes=grant << 20),
        **kwargs,
    )


def begin(source, target, sem):
    copy = pltpu.make_async_copy(source, target, sem)
    copy.start()
    return copy


def hdot(a, b, contract):
    return lax.dot_general(a, b, (contract, ((), ())), precision=HIGH, preferred_element_type=F32)


def first_half(shape):
    return lax.broadcasted_iota(jnp.int32, shape, len(shape) - 1) < 64


def columns(ref, start, size):
    lead = (slice(None),) * (len(ref.shape) - 1)
    return ref.at[lead + (slice(start, start + size),)]


def quarter_tile(quarter, tile, rows, grad, error):
    odd = lax.rem(quarter, 2)
    first = pl.multiple_of(tile * 512 + (quarter // 2) * 128, 128)
    low, high = pl.ds(first, 128), pl.ds(first + 256, 128)
    low = grad[0, rows, low].astype(F32) + error[0, rows, low].astype(F32)
    high = grad[0, rows, high].astype(F32) + error[0, rows, high].astype(F32)
    return jnp.where(first_half(low.shape), pltpu.roll(low, 64 * odd, 1), pltpu.roll(high, 64 * (1 - odd), 1))


def quarters_kernel(jobs, sizes, grad_in, error_in, *rest):
    count = len(sizes)
    outs, (grad, error), stages = rest[:count], rest[count : count + 2], rest[count + 2 : -2]
    in_sems, out_sems = rest[-2:]
    arrive = []
    for piece in range(4):
        arrive.append(begin(columns(grad_in, piece * 2048, 2048), columns(grad, piece * 2048, 2048), in_sems.at[0, piece]))
        arrive.append(begin(columns(error_in, piece * 2048, 2048), columns(error, piece * 2048, 2048), in_sems.at[1, piece]))
    leave = []
    for piece in range(4):
        arrive[2 * piece].wait()
        arrive[2 * piece + 1].wait()
        for tile in range(4 * piece, 4 * piece + 4):
            cols = slice(tile * 128, tile * 128 + 128)
            for step, start, stop, out, at in jobs:
                quarter = lax.rem(lax.axis_index("x") + step, 4)
                stages[out][at : at + stop - start, cols] = quarter_tile(quarter, tile, slice(start, stop), grad, error)
        for k in range(count):
            source, target = (columns(ref[k], piece * 512, 512) for ref in (stages, outs))
            leave.append(begin(source, target, out_sems.at[k, piece]))
    for copy in leave:
        copy.wait()


def add_kernel(right, left, a, b, upper, lower):
    upper[...] = a[...] + right[...]
    lower[...] = b[...] + left[...]


def partial_kernel(home, upper, lower, out):
    out[:64] = home[:64] + upper[...]
    out[64:] = home[64:] + lower[...]


def left_kernel(home, upper, lower, mine, other, merged, out):
    first = lax.axis_index("core") == 0
    acc = jnp.zeros((256, 256), F32)
    for pair in range(8):
        cols = slice(pair * 256, pair * 256 + 256)
        value = home[:, cols] + jnp.concatenate([upper[:, cols], lower[:, cols]], 0)
        merged[:, cols] = value
        rows = jnp.concatenate(split(value), 0)
        tiles = []
        for tile in (2 * pair, 2 * pair + 1):
            here, there = mine[tile], other[tile]
            tiles += [jnp.where(first, here, there), jnp.where(first, there, here)]
        acc += dot(rows, jnp.concatenate(split(jnp.concatenate(tiles, 0)), 1))
    acc = acc[:128] + acc[128:]
    out[...] = acc[:, :128] + acc[:, 128:]


def stacked(matrix):
    high, low = split(matrix)
    return jnp.concatenate(
        [jnp.concatenate([high, high], 1), jnp.concatenate([low, jnp.zeros_like(low)], 1)], 0
    )


def raw_kernel(p0, p1, p2, p3, merged, own, away, left_out):
    left = total([p0[...], p1[...], p2[...], p3[...]]) * 0.25
    left_out[...] = left
    turned = left.T
    turned = jnp.where(lax.axis_index("core") == 0, turned, jnp.concatenate([turned[64:], turned[:64]], 0))
    rows = stacked(turned)
    gram = lax.dot(turned, left, precision=HIGH, preferred_element_type=F32)
    for step in range(4):
        y = lax.rem(lax.axis_index("y") + step, 4)
        for pair in range(2):
            cols = [pl.ds(pl.multiple_of((4 * z + y) * 128, 128), 128) for z in (2 * pair, 2 * pair + 1)]
            block = jnp.concatenate([merged[:, c] for c in cols], 1)
            block = dot(rows, jnp.concatenate(split(block), 0))
            block = block[:128] + block[128:]
            for k in range(2):
                own[step * 5 + 2 * pair + k] = block[:64, k * 128 : k * 128 + 128]
                away[step * 5 + 2 * pair + k] = block[64:, k * 128 : k * 128 + 128]
        own[step * 5 + 4] = gram[:64]
        away[step * 5 + 4] = gram[64:]


def pack_kernel(own, came, *outs):
    for step in range(4):
        outs[step][...] = own[5 * step : 5 * step + 5] + came[5 * step : 5 * step + 5]


def sum_kernel(p0, p1, p2, p3, out):
    out[...] = total([p0[...], p1[...], p2[...], p3[...]])


def split_kernel(p0, p1, p2, p3, tiles, gram):
    whole = total([p0[...], p1[...], p2[...], p3[...]])
    tiles[...] = whole[:4] * 0.25
    gram[...] = whole[4]


def gather_kernel(p0, p1, p2, p3, out):
    for part, step in ((p0, 0), (p1, 2), (p2, 3), (p3, 1)):
        y = lax.rem(lax.axis_index("y") + step, 4)
        for z in range(4):
            out[z, y] = part[z]


def pair_up(raw, quarters, second):
    lower = first_half((128, 128))
    first, last = (raw[q] for q in quarters)
    if second:
        return jnp.where(lower, pltpu.roll(first, 64, 1), last)
    return jnp.where(lower, first, pltpu.roll(last, 64, 1))


def eliminate(work, starts, size=32):
    below = lax.broadcasted_iota(jnp.int32, (size, 1), 0)
    lane = lax.broadcasted_iota(jnp.int32, (size, 128), 1)
    for start in starts:
        stop = start + size
        panel = work[start:stop, :]
        scales = []
        for j in range(size):
            scale = 1.0 / panel[j : j + 1, start + j : start + j + 1]
            column = jnp.where(below > j, panel[:, start + j : start + j + 1] * scale, 0.0)
            panel = panel - column * panel[j : j + 1, :]
            scales.append(scale)
        scale = jnp.concatenate(scales, 0)
        work[start:stop, :] = panel * lax.sqrt(scale)
        if stop < 128:
            steps = jnp.where(lane >= stop, panel[:, :128] * scale, 0.0)
            work[stop:, :] = work[stop:, :] - hdot(steps, panel, ((0,), (0,)))[stop:]


def begin_factor_kernel(gram, came, work):
    first = lax.axis_index("core") == 0
    gram, came = gram[...], came[...]
    gram = jnp.concatenate([jnp.where(first, gram, came), jnp.where(first, came, gram)], 0)
    row = lax.broadcasted_iota(jnp.int32, (128, 128), 0)
    diagonal = row == lax.broadcasted_iota(jnp.int32, (128, 128), 1)
    eye = jnp.where(diagonal, 1.0, 0.0)
    trace = jnp.sum(jnp.where(diagonal, gram, 0.0))
    work[:, :128] = gram + 1e-06 * trace / 128 * eye
    work[:, 128:] = eye
    eliminate(work, (0,))


def next_factor_kernel(begun, work):
    work[...] = begun[...]
    eliminate(work, (32, 64))


def end_factor_kernel(begun, left, factor, inverse, work):
    work[...] = begun[...]
    eliminate(work, (96,))
    lower = work[:, 128:]
    inverse[...] = lower
    factor[...] = hdot(hdot(left[...], lower, ((1,), (1,))), lower, ((1,), (0,)))


def last_kernel(factor, inverse, *rest):
    raws, (grad, error, momentum, params), outs, right = rest[:8], rest[8:12], rest[12:15], rest[15]
    stages, sems = rest[16:19], rest[19]
    x, z, y = (lax.axis_index(axis) for axis in ("x", "z", "y"))
    first, odd, late = lax.axis_index("core") == 0, lax.rem(x, 2) == 1, x >= 2

    def quarters_of(part, place):
        here, after, before, far = (
            jnp.concatenate([raws[k][part, place], raws[4 + k][part, place]], 0) for k in range(4)
        )
        own = jnp.where(odd, before, here), jnp.where(odd, here, after)
        return own, (jnp.where(odd, after, far), jnp.where(odd, far, before))

    def columns_of(own, other, second):
        own, other = pair_up(own, (0, 1), second), pair_up(other, (0, 1), second)
        return jnp.where(late, other, own), jnp.where(late, own, other)

    weights = factor[...]
    high, low = split(jnp.where(first, weights, pltpu.roll(weights, 64, 1)))
    rows = jnp.concatenate([high, high, low], 1)
    leave = []
    for part in range(4):
        for place in range(4):
            own, other = quarters_of(part, place)
            for run in range(2):
                block = jnp.concatenate(columns_of(own, other, run == 1), 1)
                high, low = split(block)
                approx = dot(rows, jnp.concatenate([high, low, high], 0))
                start = part * 2048 + place * 512 + run * 256
                cols = slice(start, start + 256)
                merged = grad[0, :, cols].astype(F32) + error[0, :, cols].astype(F32)
                stages[0][0, :, cols] = (merged - approx).astype(BF16)
                moment = 0.9 * momentum[:, cols].astype(F32) + approx
                stages[1][:, cols] = moment.astype(BF16)
                stages[2][:, cols] = params[:, cols] - 0.7 * (approx + 0.9 * moment)
            if place % 2 == 1:
                for k in range(3):
                    start = part * 2048 + (place - 1) * 512
                    source, target = (columns(ref[k], start, 1024) for ref in (stages, outs))
                    leave.append(begin(source, target, sems.at[k, 2 * part + place // 2]))
    own, other = quarters_of(z, y)
    own, other = (
        tuple(jnp.where(first, tile, jnp.concatenate([tile[64:], tile[:64]], 0)) for tile in pair)
        for pair in (own, other)
    )
    halves = zip(columns_of(own, other, False), columns_of(own, other, True))
    for k, (low, high) in enumerate(halves):
        block = hdot(inverse[...], jnp.where(first, low, high), ((1,), (0,)))
        right[k * 128 : k * 128 + 128, :] = block.T
    for copy in leave:
        copy.wait()


def quarters(jobs, sizes, grad, error):
    shapes = [(size, 2048) for size in sizes]
    return call(
        functools.partial(quarters_kernel, jobs, sizes),
        tuple(jax.ShapeDtypeStruct(shape, F32) for shape in shapes),
        [ANY, ANY],
        (ANY,) * len(shapes),
        us=4,
        grant=GRANT,
        scratch_shapes=[pltpu.VMEM((1, 128, 8192), BF16)] * 2
        + [pltpu.VMEM(shape, F32) for shape in shapes]
        + [pltpu.SemaphoreType.DMA((2, 4)), pltpu.SemaphoreType.DMA((len(shapes), 4))],
    )(grad, error)


def local(grad, error, momentum, params, right_factor):
    x = lax.axis_index("x")
    square = jax.ShapeDtypeStruct((128, 128), F32)
    tiles = lambda n: jax.ShapeDtypeStruct((n, 64, 128), F32)

    half, whole = (jax.ShapeDtypeStruct((rows, 2048), F32) for rows in (64, 128))
    a2, b2, b1, a3 = quarters(
        ((2, 0, 64, 0, 0), (2, 64, 128, 1, 0), (1, 64, 128, 2, 0), (3, 0, 64, 3, 0)), (64,) * 4, grad, error
    )
    far_a, far_b = ring(a2, "x", 1), ring(b2, "x", -1)
    b_right, a_left = ring(b1, "x", 1), ring(a3, "x", -1)
    home, a1, b3 = quarters(((0, 0, 128, 0, 0), (1, 0, 64, 1, 0), (3, 64, 128, 2, 0)), (128, 64, 64), grad, error)
    far_a, far_b, home, a1, b3 = lax.optimization_barrier((far_a, far_b, home, a1, b3))
    a1, b3 = call(add_kernel, (half, half), [VMEM] * 4, (VMEM,) * 2, us=0.6)(far_a, far_b, a1, b3)
    a_right, b_left = ring(a1, "x", 1), ring(b3, "x", -1)
    home = call(partial_kernel, whole, [VMEM] * 3, VMEM, us=30)(home, a_left, b_right)

    rows = lax.dynamic_slice_in_dim(right_factor, x * 64, 64, 0)
    mine = lax.all_to_all(jnp.broadcast_to(rows[None], (16, 64, 128)), PLANE, 0, 0)
    other = ring(mine, "core", 1)

    merged, part = call(left_kernel, (whole, square), [VMEM] * 5, (VMEM,) * 2, us=1.2)(
        home, a_right, b_left, mine, other
    )
    parts = exchange(part, "x")
    own, away, left_factor = call(raw_kernel, (tiles(20), tiles(20), square), [VMEM] * 5, (VMEM,) * 3, us=1)(*parts, merged)
    came = ring(away, "core", 1)

    outs = call(pack_kernel, (tiles(5),) * 4, [VMEM] * 2, (VMEM,) * 4, us=0.3)(own, came)
    outs = (outs[0], ring(outs[2], "y", 2), ring(outs[1], "y", 1), ring(outs[3], "y", -1))
    part = call(sum_kernel, tiles(5), [VMEM] * 4, VMEM, us=0.2)(*outs)
    mine, gram = call(split_kernel, (tiles(4), jax.ShapeDtypeStruct((64, 128), F32)), [VMEM] * 4, (VMEM,) * 2, us=0.2)(
        *exchange(part, "z")
    )

    gram_other = ring(gram, "core", 1)
    parts = exchange(mine, "y")
    mine, gram_other = lax.optimization_barrier((mine, gram_other))
    opposite = ring(mine, "x", 2)
    work = call(begin_factor_kernel, jax.ShapeDtypeStruct((128, 256), F32), [VMEM] * 2, VMEM, us=3.4)(gram, gram_other)
    *parts, opposite, work = lax.optimization_barrier((*parts, opposite, work))
    own = call(gather_kernel, jax.ShapeDtypeStruct((4, 4, 64, 128), F32), [VMEM] * 4, VMEM, us=0.3)(*parts)
    before, after = ring(own, "x", 1), ring(own, "x", -1)
    own_sibling, opposite = lax.optimization_barrier((ring(own, "core", 1), opposite))
    opposite = exchange(opposite, "y")
    own, work = lax.optimization_barrier((own, work))
    block = jax.ShapeDtypeStruct((128, 256), F32)
    work = call(next_factor_kernel, block, [VMEM], VMEM, us=6.2)(work)
    *opposite, work = lax.optimization_barrier((*opposite, work))
    opposite = call(gather_kernel, jax.ShapeDtypeStruct((4, 4, 64, 128), F32), [VMEM] * 4, VMEM, us=0.3)(*opposite)
    opposite_sibling = ring(opposite, "core", 1)
    factor, inverse = call(
        end_factor_kernel, (square, square), [VMEM] * 2, (VMEM,) * 2, us=3.4, scratch_shapes=[pltpu.VMEM((128, 256), F32)]
    )(work, left_factor)
    before, after, opposite_sibling, factor, inverse = lax.optimization_barrier(
        (before, after, opposite_sibling, factor, inverse)
    )
    raws = (own, after, before, opposite)
    siblings = (own_sibling, ring(after, "core", 1), ring(before, "core", 1), opposite_sibling)

    return call(
        last_kernel,
        tuple(jax.ShapeDtypeStruct(array.shape, array.dtype) for array in (error, momentum, params))
        + (jax.ShapeDtypeStruct((256, 128), F32),),
        [VMEM] * 14,
        (ANY,) * 3 + (VMEM,),
        us=7,
        grant=20,
        scratch_shapes=[
            pltpu.VMEM((1, 128, 8192), BF16),
            pltpu.VMEM((128, 8192), BF16),
            pltpu.VMEM((128, 8192), F32),
            pltpu.SemaphoreType.DMA((3, 8)),
        ],
    )(factor, inverse, *raws, *siblings, grad, error, momentum, params)


def solution(mesh):
    fine = Mesh(mesh.devices.reshape(4, 4, 4, 2), ("x", "z", "y", "core"))
    shard = ("z", "y", "core")
    return jax.shard_map(
        local,
        mesh=fine,
        in_specs=(P("x", shard, None), P("x", shard, None), P(shard, None), P(shard, None), P(shard, None)),
        out_specs=(P("x", shard, None), P(shard, None), P(shard, None), P(shard, None)),
        check_vma=False,
    )
```
